128 devices in a mesh: ctx: 8 (over x, y_hi), tp: 16 (over z, y_lo, core).
Axes of the slice: x: 4, y: 4 (y_hi: 2, y_lo: 2; y = y_hi * 2 + y_lo), z: 4, core: 2. Of those that a mesh axis runs over, the one named last changes fastest.
Arguments:
- pre_queries: bfloat16 [2048, 24576], P('ctx', 'tp'), may hold values from -256 to 256
- pre_latent: bfloat16 [2048, 576], P(('ctx', 'tp')), may hold values from -6 to 6
- absorb_keys: bfloat16 [512, 16384], P(None, 'tp'), may hold values from -0.25 to 0.25
- absorb_values: bfloat16 [512, 16384], P(None, 'tp'), may hold values from -0.75 to 0.75
- step_queries: bfloat16 [4, 256, 24576], P(None, 'ctx', 'tp'), may hold values from -256 to 256
- step_latent: bfloat16 [4, 256, 576], P(None, 'ctx'), may hold values from -6 to 6
- context_lengths: int32 [256], P('ctx'), may hold values from 1 to 2048, as said below
- page_table: int32 [256, 32], P('ctx'), may hold values from 0 to 31, each once within a row
- out_weight: bfloat16 [16384, 7168], P('tp'), may hold values from -0.046875 to 0.046875
Outputs:
- prefill_heads: bfloat16 [2048, 16384], P('ctx', 'tp')
- decode_out: bfloat16 [4, 256, 7168], P(None, 'ctx', 'tp')
The draws below stay inside these ranges and needn't reach their ends.
Inputs may be any that keep to these rules, and one draw needn't show every extreme that they name: `context_lengths`: at least one decode row has the whole pool in its context. `page_table`: each row lists every page of the pool once.
All inputs are finite; a program needn't handle non-finite values.
Results may differ from the reference program's by a relative error of at most 0.024.
Values may be sent and summed in bfloat16 or wider, within the bound.
No kernel may reach another device: no remote copies, remote signals or barrier semaphores. Data moves between devices by JAX's collectives and lax.ppermute only.
A program may use at most 128 MiB of HBM per device.

```python
import math
import jax
import jax.numpy as jnp
from jax import lax

HEADS = 128
LATENT = 512
ROPE = 64
NOPE = 128
VALUE_DIM = 128
MODEL = 7168
PAGE = 64
STEPS = 4
PRE = 2048
PAGES = 32
ROWS = 256


def draw_pre_latent(key, part):
    key = jax.random.fold_in(key, 1)
    values = jnp.clip(jax.random.normal(key, (PRE, LATENT + ROPE), jnp.float32), -6.0, 6.0)
    return values.astype(jnp.bfloat16)


def draw_pre_queries(key, part):
    key = jax.random.fold_in(key, 2)
    values = jnp.clip(jax.random.normal(key, (PRE, HEADS * (NOPE + ROPE)), jnp.float32), -6.0, 6.0)
    return values.astype(jnp.bfloat16)


def draw_step_queries(key, part):
    key = jax.random.fold_in(key, 3)
    values = jnp.clip(jax.random.normal(key, (STEPS, ROWS, HEADS * (NOPE + ROPE)), jnp.float32), -6.0, 6.0)
    return values.astype(jnp.bfloat16)


def draw_step_latent(key, part):
    key = jax.random.fold_in(key, 4)
    values = jnp.clip(jax.random.normal(key, (STEPS, ROWS, LATENT + ROPE), jnp.float32), -6.0, 6.0)
    return values.astype(jnp.bfloat16)


def draw_context_lengths(key, part):
    key = jax.random.fold_in(key, 5)
    first = jax.random.randint(jax.random.fold_in(key, 1), (ROWS,), 1, PRE + 1)
    second = jax.random.randint(jax.random.fold_in(key, 2), (ROWS,), 1, PRE + 1)
    chosen = jax.random.randint(jax.random.fold_in(key, 3), (), 0, ROWS)
    lengths = jnp.minimum(first, second)
    lengths = jnp.where(jnp.arange(ROWS) == chosen, PRE, lengths)
    return lengths.astype(jnp.int32)


def block_scale(key, extent, shards, least, top_value):
    def one(position, shards_of):
        heights = jax.random.uniform(jax.random.fold_in(jax.random.fold_in(key, 6), position), (shards_of,), jnp.float32, least / len(shards), top_value / len(shards))
        return jnp.repeat(jnp.exp(heights), extent[position] // shards_of).reshape((-1,) + (1,) * (len(extent) - position - 1))

    gain = one(*shards[0])
    for cut in shards[1:]:
        gain = gain * one(*cut)
    return gain


def normal_values(key, shape, scale, most, shards=(), held_as=jnp.bfloat16):
    level = block_scale(key, shape, shards, -0.22, 0.18) if shards else 1.0
    result = jax.random.normal(key, shape, jnp.float32) * scale * level
    return jnp.minimum(jnp.maximum(result, -most), most).astype(held_as)


def setup_inputs(seed: int = 0) -> dict:
    splits = jax.random.split(jax.random.key(seed), 10)
    pre_queries = draw_pre_queries(jax.random.fold_in(splits[9], 71), 0)
    pre_latent = draw_pre_latent(jax.random.fold_in(splits[9], 71), 0)
    absorb_keys = normal_values(splits[2], (LATENT, HEADS * NOPE), LATENT ** -0.5, 0.25, ((1, 16),))
    absorb_values = normal_values(splits[3], (LATENT, HEADS * VALUE_DIM), 64 ** -0.5, 0.75, ((1, 16),))
    step_queries = draw_step_queries(jax.random.fold_in(splits[9], 71), 0)
    step_latent = draw_step_latent(jax.random.fold_in(splits[9], 71), 0)
    context_lengths = draw_context_lengths(jax.random.fold_in(splits[9], 71), 0)
    page_table = jax.vmap(lambda own: jax.random.permutation(own, PAGES))(jax.random.split(splits[7], ROWS)).reshape((ROWS, PAGES)).astype(jnp.int32)
    out_weight = normal_values(splits[8], (HEADS * VALUE_DIM, MODEL), (HEADS * VALUE_DIM) ** -0.5, 0.046875, ((0, 16),))
    return dict(pre_queries=pre_queries, pre_latent=pre_latent, absorb_keys=absorb_keys, absorb_values=absorb_values, step_queries=step_queries, step_latent=step_latent, context_lengths=context_lengths, page_table=page_table, out_weight=out_weight)


def reference(pre_queries, pre_latent, absorb_keys, absorb_values, step_queries, step_latent, context_lengths, page_table, out_weight):
    width = NOPE + ROPE
    scale = 1.0 / math.sqrt(NOPE + ROPE)
    key_map = absorb_keys.reshape(LATENT, HEADS, NOPE).transpose(1, 0, 2)
    value_map = absorb_values.reshape(LATENT, HEADS, VALUE_DIM).transpose(1, 0, 2)
    latent_part = pre_latent[:, :LATENT]
    positions = jnp.arange(PRE)
    causal = positions[None, :] <= positions[:, None]

    def join_query(query, key_rows):
        absorbed = jnp.dot(query[:, :NOPE], key_rows.T, preferred_element_type=jnp.float32).astype(jnp.bfloat16)
        return jnp.concatenate([absorbed, query[:, NOPE:]], axis=1)

    def prefill_head(items):
        query, key_rows, value_rows = items
        joined = join_query(query, key_rows)
        scores = jnp.dot(joined, pre_latent.T, preferred_element_type=jnp.float32) * scale
        largest = lax.optimization_barrier(jnp.max(jnp.where(causal, scores, -jnp.inf), axis=1, keepdims=True))
        expo = jnp.where(causal, jnp.exp(scores - largest), 0.0)
        total = lax.optimization_barrier(jnp.sum(expo, axis=1, keepdims=True))
        mixed = (jnp.dot(expo.astype(jnp.bfloat16), latent_part, preferred_element_type=jnp.float32) / total).astype(jnp.bfloat16)
        return jnp.dot(mixed, value_rows, preferred_element_type=jnp.float32).astype(jnp.bfloat16)
    head_queries = pre_queries.reshape(PRE, HEADS, width).transpose(1, 0, 2)
    prefill_out = lax.map(prefill_head, (head_queries, key_map, value_map))
    prefill_heads = prefill_out.transpose(1, 0, 2).reshape(PRE, HEADS * VALUE_DIM)
    page_ids = jnp.arange(PAGES)
    matches = page_table[:, :, None] == page_ids[None, None, :]
    slot = lax.optimization_barrier(jnp.sum(jnp.where(matches, page_ids[None, :, None], 0), axis=1))
    place = (slot[:, :, None] * PAGE + jnp.arange(PAGE)[None, None, :]).reshape(ROWS, PRE)
    visible = place < context_lengths[:, None]
    outputs = []
    for step in range(STEPS):
        new_keys = step_latent[:step + 1]

        def decode_head(items):
            query, key_rows, value_rows = items
            joined = join_query(query, key_rows)
            pool_scores = jnp.dot(joined, pre_latent.T, preferred_element_type=jnp.float32) * scale
            new_scores = jnp.einsum('rk,jrk->rj', joined.astype(jnp.float32), new_keys.astype(jnp.float32)) * scale
            largest = jnp.maximum(lax.optimization_barrier(jnp.max(jnp.where(visible, pool_scores, -jnp.inf), axis=1)), lax.optimization_barrier(jnp.max(new_scores, axis=1)))
            pool_expo = jnp.where(visible, jnp.exp(pool_scores - largest[:, None]), 0.0)
            new_expo = jnp.exp(new_scores - largest[:, None])
            total = lax.optimization_barrier(jnp.sum(pool_expo, axis=1)) + lax.optimization_barrier(jnp.sum(new_expo, axis=1))
            numerator = jnp.dot(pool_expo.astype(jnp.bfloat16), latent_part, preferred_element_type=jnp.float32)
            numerator = numerator + jnp.einsum('rj,jrk->rk', new_expo.astype(jnp.bfloat16).astype(jnp.float32), new_keys[:, :, :LATENT].astype(jnp.float32))
            mixed = (numerator / total[:, None]).astype(jnp.bfloat16)
            return jnp.dot(mixed, value_rows, preferred_element_type=jnp.float32).astype(jnp.bfloat16)
        queries = step_queries[step].reshape(ROWS, HEADS, width).transpose(1, 0, 2)
        heads_out = lax.map(decode_head, (queries, key_map, value_map))
        heads_out = heads_out.transpose(1, 0, 2).reshape(ROWS, HEADS * VALUE_DIM)
        outputs.append(jnp.dot(heads_out, out_weight, preferred_element_type=jnp.float32).astype(jnp.bfloat16))
    return (prefill_heads, jnp.stack(outputs))
```

```python
import functools
import itertools
import math

import jax
import jax.numpy as jnp
from jax import lax
from jax.experimental import pallas as pl
from jax.experimental.pallas import tpu as pltpu
from jax.sharding import PartitionSpec as P

LATENT = 512
ROPE = 64
NOPE = 128
VALUE_DIM = 128
PAGE = 64
STEPS = 4
WIDTH = LATENT + ROPE
HEAD = NOPE + ROPE
HEADS = 8
TOKENS = 256
ROWS = 32
QUERIES = STEPS * ROWS
HALF = 1024
POOL = 2 * HALF
MODEL = 7168
SHARE = 448
BOTH = ("ctx", "tp")

hidden = -1e30
to_exp2 = math.log2(math.e) / math.sqrt(HEAD)
vmem = pl.BlockSpec(memory_space=pltpu.VMEM)
smem = pl.BlockSpec(memory_space=pltpu.SMEM)
anywhere = pl.BlockSpec(memory_space=pl.ANY)
params = pltpu.CompilerParams(vmem_limit_bytes=56 * 1024 * 1024)


def flat(x, y, z, core):
    return (x * 2 + y // 2) * 16 + z * 4 + (y % 2) * 2 + core


def chips():
    return itertools.product(range(4), range(4), range(4), range(2))


def other_core():
    return [(flat(x, y, z, c), flat(x, y, z, 1 - c)) for x, y, z, c in chips()]


def to_group(dz, dy):
    return [(flat(x, y, z, c), flat(x, y ^ dy, (z + dz) % 4, c)) for x, y, z, c in chips()]


def same_core_groups():
    return [
        [
            flat(x, yh * 2 + yl, z, core)
            for x, yh, z, yl in itertools.product(range(4), range(2), range(4), range(2))
        ]
        for core in range(2)
    ]


def dot(a, b):
    return jnp.dot(a, b, preferred_element_type=jnp.float32)


def dot_t(a, b):
    return lax.dot_general(a, b, (((1,), (1,)), ((), ())), preferred_element_type=jnp.float32)


def absorb_kernel(pre_ref, step_ref, key_ref, pre_out, step_out):
    for source, out in ((pre_ref, pre_out), (step_ref, step_out)):
        for pair in range(HEADS // 2):
            both = source[:, pair * 2 * HEAD : (pair + 1) * 2 * HEAD]
            for part in range(2):
                head = pair * 2 + part
                query = both[:, part * HEAD : (part + 1) * HEAD]
                key_map = key_ref[:, head * NOPE : (head + 1) * NOPE]
                out[head, :, :LATENT] = dot_t(query[:, :NOPE], key_map).astype(jnp.bfloat16)
                out[head, :, LATENT:] = query[:, NOPE:]


def absorb(pre_queries, step_queries, absorb_keys):
    return pl.pallas_call(
        absorb_kernel,
        out_shape=(
            jax.ShapeDtypeStruct((HEADS, TOKENS, WIDTH), jnp.bfloat16),
            jax.ShapeDtypeStruct((HEADS, QUERIES, WIDTH), jnp.bfloat16),
        ),
        in_specs=[vmem] * 3,
        out_specs=(vmem, vmem),
        compiler_params=params,
        cost_estimate=pl.CostEstimate(
            flops=2 * 3072 * 128 * 512, bytes_accessed=6_000_000, transcendentals=0
        ),
        name="absorb",
    )(pre_queries, step_queries, absorb_keys)


def softmax_rows(scores, bias_ref, weights, bias_rows, block):
    rows = scores.shape[0]
    inverse = []
    for start in range(0, rows, block):
        shifted = (
            scores[start : start + block, :]
            + bias_ref[start % bias_rows : start % bias_rows + block, :]
        )
        largest = jnp.max(shifted, axis=1, keepdims=True)
        expo = jnp.exp2(shifted * to_exp2 - largest * to_exp2)
        inverse.append(1.0 / jnp.sum(expo, axis=1, keepdims=True))
        weights[start : start + block, :] = expo.astype(jnp.bfloat16)
    return jnp.concatenate(inverse, axis=0)


def attend(count, queries, keys, bias_ref, scores, weights, emit, bias_rows, block):
    def score(i, slot):
        query = queries[i]
        at = 0
        for ref in keys:
            size = ref.shape[0]
            scores[slot, :, at : at + size] = dot_t(query, ref[...])
            at += size

    def finish(i, slot):
        inverse = softmax_rows(scores.at[slot], bias_ref, weights, bias_rows, block)
        total = None
        at = 0
        for ref in keys:
            size = ref.shape[0]
            term = dot(weights[:, at : at + size], ref[:, :LATENT])
            total = term if total is None else total + term
            at += size
        emit(i, (total * inverse).astype(jnp.bfloat16))

    score(0, 0)

    def step(i, carry):
        slot = lax.rem(i, 2)
        score(i + 1, 1 - slot)
        finish(i, slot)
        return carry

    lax.fori_loop(0, count - 1, step, 0)
    finish(count - 1, (count - 1) % 2)


def token_in_half(shape, dim, core):
    row = lax.broadcasted_iota(jnp.int32, shape, dim)
    return (row // 16) * 32 + core * 16 + row % 16


def prefill_kernel(info, queries, first, second, value_ref, out_ref, bias, scores, weights):
    ctx, core = info[0], info[1]
    query = ctx * TOKENS + lax.broadcasted_iota(jnp.int32, (TOKENS, HALF), 0)
    for half in range(2):
        token = token_in_half((TOKENS, HALF), 1, core if half == 0 else 1 - core)
        bias[:, half * HALF : (half + 1) * HALF] = jnp.where(token <= query, 0.0, hidden)

    def emit(i, mixed):
        columns = pl.ds(pl.multiple_of(i * VALUE_DIM, VALUE_DIM), VALUE_DIM)
        out_ref[:, columns] = dot(mixed, value_ref[:, columns]).astype(jnp.bfloat16)

    attend(HEADS, queries, [first, second], bias, scores, weights, emit, TOKENS, 32)


def prefill(info, queries, first, second, absorb_values):
    return pl.pallas_call(
        prefill_kernel,
        out_shape=jax.ShapeDtypeStruct((TOKENS, HEADS * VALUE_DIM), jnp.bfloat16),
        in_specs=[smem] + [vmem] * 4,
        out_specs=vmem,
        scratch_shapes=[
            pltpu.VMEM((TOKENS, POOL), jnp.float32),
            pltpu.VMEM((2, TOKENS, POOL), jnp.float32),
            pltpu.VMEM((TOKENS, POOL), jnp.bfloat16),
        ],
        compiler_params=params,
        cost_estimate=pl.CostEstimate(
            flops=2 * 2048 * 2048 * 1088, bytes_accessed=6_000_000, transcendentals=2048 * 2048
        ),
        name="prefill",
    )(info, queries, first, second, absorb_values)


def decode_kernel(
    info, queries, first, second, newest, limit_ref, value_ref, weight_hbm,
    out_ref, bias, scores, weights, heads_out, weight, sem,
):
    core, z, yl = info[1], info[2], info[3]
    load = pltpu.make_async_copy(weight_hbm, weight, sem)
    load.start()
    limit = limit_ref[...]
    for half in range(2):
        token = token_in_half((QUERIES, HALF), 1, core if half == 0 else 1 - core) % PAGE
        page = lax.broadcasted_iota(jnp.int32, (ROWS, HALF), 0)
        of = lax.broadcasted_iota(jnp.int32, (ROWS, HALF), 1) // (PAGE // 2)
        spread = dot(limit, (page == of).astype(jnp.bfloat16))
        bias[:, half * HALF : (half + 1) * HALF] = jnp.where(
            token.astype(jnp.float32) < spread, 0.0, hidden
        )
    mine = lax.broadcasted_iota(jnp.int32, (QUERIES, QUERIES), 0)
    theirs = lax.broadcasted_iota(jnp.int32, (QUERIES, QUERIES), 1)
    seen = (mine % ROWS == theirs % ROWS) & (theirs // ROWS <= mine // ROWS)
    bias[:, POOL:] = jnp.where(seen, 0.0, hidden)

    def emit(i, mixed):
        for part in range(2):
            columns = pl.ds(pl.multiple_of((i * 2 + part) * VALUE_DIM, VALUE_DIM), VALUE_DIM)
            rows = mixed[part * QUERIES : (part + 1) * QUERIES]
            heads_out[:, columns] = dot(rows, value_ref[:, columns]).astype(jnp.bfloat16)

    attend(HEADS // 2, queries, [first, second, newest], bias, scores, weights, emit, QUERIES, 32)
    load.wait()

    def project(pair, carry):
        columns = pl.ds(pl.multiple_of(pair * 2 * SHARE, 2 * SHARE), 2 * SHARE)
        term = dot(heads_out[...], weight[:, columns])
        turned = term.T.astype(jnp.bfloat16)
        place = lax.rem(pair // 2 - z + 4, 4) * 2 + lax.rem(pair + yl, 2)
        out_ref[core, place] = turned[:SHARE]
        out_ref[1 - core, place] = turned[SHARE:]
        return carry

    lax.fori_loop(0, MODEL // (2 * SHARE), project, 0)


def decode(info, queries, first, second, newest, limit, absorb_values, out_weight):
    keys = POOL + QUERIES
    return pl.pallas_call(
        decode_kernel,
        out_shape=jax.ShapeDtypeStruct((2, 8, SHARE, QUERIES), jnp.bfloat16),
        in_specs=[smem] + [vmem] * 6 + [anywhere],
        out_specs=vmem,
        scratch_shapes=[
            pltpu.VMEM((QUERIES, keys), jnp.float32),
            pltpu.VMEM((2, 2 * QUERIES, keys), jnp.float32),
            pltpu.VMEM((2 * QUERIES, keys), jnp.bfloat16),
            pltpu.VMEM((QUERIES, HEADS * VALUE_DIM), jnp.bfloat16),
            pltpu.VMEM((HEADS * VALUE_DIM, MODEL), jnp.bfloat16),
            pltpu.SemaphoreType.DMA(()),
        ],
        compiler_params=params,
        cost_estimate=pl.CostEstimate(
            flops=2 * 1024 * 2176 * 1088 + 2 * 128 * 1024 * 7168,
            bytes_accessed=22_000_000,
            transcendentals=1024 * 2176,
        ),
        name="decode",
    )(info, queries, first, second, newest, limit, absorb_values, out_weight)


def on_device(
    pre_queries,
    pre_latent,
    absorb_keys,
    absorb_values,
    step_queries,
    step_latent,
    context_lengths,
    page_table,
    out_weight,
):
    tp = lax.axis_index("tp")
    core, yl, z = tp % 2, (tp // 2) % 2, tp // 4
    info = jnp.stack([lax.axis_index("ctx"), core, z, yl]).astype(jnp.int32)
    pre_joined, step_joined = absorb(
        pre_queries, step_queries.reshape(QUERIES, HEADS * HEAD), absorb_keys
    )
    pages = page_table.shape[1]
    page_ids = jnp.arange(pages, dtype=jnp.int32)
    matches = page_table[:, :, None] == page_ids[None, None, :]
    slot = jnp.sum(jnp.where(matches, page_ids[None, :, None], 0), axis=1)
    limit = jnp.clip(context_lengths[:, None] - slot * PAGE, 0, PAGE).astype(jnp.bfloat16)
    limit = jnp.tile(limit, (STEPS, 1))

    first = lax.all_to_all(
        jnp.broadcast_to(pre_latent[None], (64, 16, WIDTH)),
        BOTH,
        0,
        0,
        axis_index_groups=same_core_groups(),
    ).reshape(HALF, WIDTH)
    second = lax.ppermute(first, BOTH, other_core())

    shares = decode(
        info,
        step_joined.reshape(HEADS // 2, 2 * QUERIES, WIDTH),
        first,
        second,
        step_latent.reshape(QUERIES, WIDTH),
        limit,
        absorb_values,
        out_weight,
    )
    arrived = lax.ppermute(shares[1], BOTH, other_core())
    chip = (shares[0].astype(jnp.float32) + arrived.astype(jnp.float32)).astype(jnp.bfloat16)
    total = chip[0].astype(jnp.float32)
    for place in range(1, 8):
        got = lax.ppermute(chip[place], BOTH, to_group(place // 2, place % 2))
        total = total + got.astype(jnp.float32)
    decode_out = total.astype(jnp.bfloat16).T.reshape(STEPS, ROWS, SHARE)

    prefill_heads = prefill(info, pre_joined, first, second, absorb_values)
    return (prefill_heads, decode_out)


def solution(mesh):
    return jax.shard_map(
        on_device,
        mesh=mesh,
        in_specs=(
            P("ctx", "tp"),
            P(("ctx", "tp"), None),
            P(None, "tp"),
            P(None, "tp"),
            P(None, "ctx", "tp"),
            P(None, "ctx", None),
            P("ctx"),
            P("ctx", None),
            P("tp", None),
        ),
        out_specs=(P("ctx", "tp"), P(None, "ctx", "tp")),
        check_vma=False,
    )
```

```python
import functools
import itertools
import math

import jax
import jax.numpy as jnp
from jax import lax
from jax.experimental import pallas as pl
from jax.experimental.pallas import tpu as pltpu
from jax.sharding import PartitionSpec as P

LATENT = 512
ROPE = 64
NOPE = 128
VALUE_DIM = 128
PAGE = 64
STEPS = 4
WIDTH = LATENT + 2 * ROPE
PIECE = 72
BLOCK = 256
HEAD = NOPE + ROPE
HEADS = 8
TOKENS = 256
ROWS = 32
QUERIES = STEPS * ROWS
POOL = 2048
KEYS = POOL + QUERIES
MODEL = 7168
SHARE = 448
BOTH = ("ctx", "tp")

hidden = -1e30
to_exp2 = math.log2(math.e) / math.sqrt(HEAD)
vmem = pl.BlockSpec(memory_space=pltpu.VMEM)
smem = pl.BlockSpec(memory_space=pltpu.SMEM)
anywhere = pl.BlockSpec(memory_space=pl.ANY)
params = pltpu.CompilerParams(vmem_limit_bytes=56 * 1024 * 1024)


def flat(x, y, z, core):
    return (x * 2 + y // 2) * 16 + z * 4 + (y % 2) * 2 + core


def chips():
    return itertools.product(range(4), range(4), range(4), range(2))


def chip_groups():
    return [
        [flat(x, yh * 2 + yl, z, core) for z, yl in itertools.product(range(4), range(2))]
        for x, yh, core in itertools.product(range(4), range(2), range(2))
    ]


def other_core():
    return [(flat(x, y, z, c), flat(x, y, z, 1 - c)) for x, y, z, c in chips()]


def same_core_groups():
    return [
        [
            flat(x, yh * 2 + yl, z, core)
            for x, yh, z, yl in itertools.product(range(4), range(2), range(4), range(2))
        ]
        for core in range(2)
    ]


def dot(a, b):
    return jnp.dot(a, b, preferred_element_type=jnp.float32)


def dot_t(a, b):
    return lax.dot_general(a, b, (((1,), (1,)), ((), ())), preferred_element_type=jnp.float32)


def pack_kernel(latent_ref, out_ref):
    latent = latent_ref[...].astype(jnp.float32)
    rope = latent[:, LATENT:]
    parts = [latent[:, at : at + 128] for at in range(0, LATENT, 128)]
    parts.append(jnp.concatenate([rope[:8], rope[8:]], axis=1))
    piece = jnp.concatenate(parts, axis=0).astype(jnp.bfloat16)
    for place in range(64):
        out_ref[place] = piece


def pack(latent):
    return pl.pallas_call(
        pack_kernel,
        out_shape=jax.ShapeDtypeStruct((64, PIECE, 128), jnp.bfloat16),
        in_specs=[vmem],
        out_specs=vmem,
        name="pack",
    )(latent)


def unpack(own, other, keys):
    for block in range(POOL // BLOCK):
        for half, source in enumerate((own, other)):
            rows = slice(block * BLOCK + half * 128, block * BLOCK + half * 128 + 128)
            pieces = slice(block * 8, block * 8 + 8)
            for tile in range(4):
                keys[rows, tile * 128 : (tile + 1) * 128] = source[
                    pieces, tile * 16 : (tile + 1) * 16, :
                ].reshape(128, 128)
            rope = source[pieces, 64:72, :].astype(jnp.float32)
            left = lax.broadcasted_iota(jnp.int32, rope.shape, 2) < ROPE
            both = jnp.concatenate([jnp.where(left, rope, 0.0), jnp.where(left, 0.0, rope)], axis=1)
            keys[rows, LATENT:] = both.reshape(128, 128).astype(jnp.bfloat16)


def token_of_key(shape, dim, core):
    row = lax.broadcasted_iota(jnp.int32, shape, dim)
    owner = jnp.where((row // 128) % 2 == 0, core, 1 - core)
    return ((row % 128) // 16) * 32 + owner * 16 + row % 16


def absorb_kernel(
    info, pre_ref, step_ref, key_ref, latent_ref, length_ref, table_ref,
    pre_out, step_out, new_out, bias,
):
    core = info[1]
    for source, out in ((pre_ref, pre_out), (step_ref, step_out)):
        for pair in range(HEADS // 2):
            both = source[:, pair * 2 * HEAD : (pair + 1) * 2 * HEAD]
            for part in range(2):
                head = pair * 2 + part
                query = both[:, part * HEAD : (part + 1) * HEAD]
                key_map = key_ref[:, head * NOPE : (head + 1) * NOPE]
                out[head, :, :LATENT] = dot_t(query[:, :NOPE], key_map).astype(jnp.bfloat16)
                rope = query[:, NOPE:]
                out[head, :, LATENT:] = jnp.concatenate([rope, rope], axis=1)
    new_out[:, : LATENT + ROPE] = latent_ref[...]
    new_out[:, LATENT + ROPE :] = jnp.zeros((QUERIES, ROPE), jnp.bfloat16)
    table = table_ref[...]
    pages = table.shape[1]
    page = lax.broadcasted_iota(jnp.int32, table.shape, 1)
    slot = jnp.zeros(table.shape, jnp.int32)
    for place in range(pages):
        slot = slot + jnp.where(table[:, place : place + 1] == page, place, 0)
    limit = jnp.clip(length_ref[...] - slot * PAGE, 0, PAGE).astype(jnp.float32)
    shape = (pages, POOL)
    key = lax.broadcasted_iota(jnp.int32, shape, 1)
    of = (key // BLOCK) * (BLOCK // PAGE) + (key % 128) // (PAGE // 2)
    owner = (lax.broadcasted_iota(jnp.int32, shape, 0) == of).astype(jnp.bfloat16)
    spread = dot(limit.astype(jnp.bfloat16), owner)
    token = (token_of_key((ROWS, POOL), 1, core) % PAGE).astype(jnp.float32)
    rows = jnp.where(token < spread, 0.0, hidden)
    for step in range(STEPS):
        bias[step * ROWS : (step + 1) * ROWS, :POOL] = rows
    mine = lax.broadcasted_iota(jnp.int32, (QUERIES, QUERIES), 0)
    theirs = lax.broadcasted_iota(jnp.int32, (QUERIES, QUERIES), 1)
    seen = (mine % ROWS == theirs % ROWS) & (theirs // ROWS <= mine // ROWS)
    bias[:, POOL:] = jnp.where(seen, 0.0, hidden)


def absorb(info, pre_queries, step_queries, absorb_keys, step_latent, lengths, table):
    return pl.pallas_call(
        absorb_kernel,
        out_shape=(
            jax.ShapeDtypeStruct((HEADS, TOKENS, WIDTH), jnp.bfloat16),
            jax.ShapeDtypeStruct((HEADS, QUERIES, WIDTH), jnp.bfloat16),
            jax.ShapeDtypeStruct((QUERIES, WIDTH), jnp.bfloat16),
            jax.ShapeDtypeStruct((QUERIES, KEYS), jnp.float32),
        ),
        in_specs=[smem] + [vmem] * 6,
        out_specs=(vmem,) * 4,
        compiler_params=params,
        cost_estimate=pl.CostEstimate(
            flops=2 * 3072 * 128 * 512, bytes_accessed=12_000_000, transcendentals=0
        ),
        name="absorb",
    )(info, pre_queries, step_queries, absorb_keys, step_latent, lengths, table)


def softmax_rows(scores, bias, weights, start, count):
    bias_start = start % bias.shape[0]
    shifted = scores[start : start + count, :] + bias[bias_start : bias_start + count, :]
    largest = jnp.max(shifted, axis=1, keepdims=True)
    expo = jnp.exp2(shifted * to_exp2 - largest * to_exp2)
    weights[start : start + count, :] = expo.astype(jnp.bfloat16)
    return 1.0 / jnp.sum(expo, axis=1, keepdims=True)


def attend(queries, keys, bias, scores, weights, emit, block=16):
    count, rows = queries.shape[0], queries.shape[1]
    parts = [(at, min(BLOCK, keys.shape[0] - at)) for at in range(0, keys.shape[0], BLOCK)]

    def score(i, out, at, size):
        out[:, at : at + size] = dot_t(queries[i], keys[at : at + size, :])

    def item(i, now, later, weight, more):
        inverse = []
        turns = rows // block
        for turn in range(turns):
            if more:
                for at, size in parts[turn * len(parts) // turns : (turn + 1) * len(parts) // turns]:
                    score(i + 1, later, at, size)
            inverse.append(softmax_rows(now, bias, weight, turn * block, block))
        inverse = jnp.concatenate(inverse, axis=0)
        mixed = [
            (dot(weight[...], keys[:, at : at + 256]) * inverse).astype(jnp.bfloat16)
            for at in range(0, LATENT, 256)
        ]
        emit(i, jnp.concatenate(mixed, axis=1))

    for at, size in parts:
        score(0, scores[0], at, size)

    def two(turn, carry):
        item(2 * turn, scores[0], scores[1], weights[0], True)
        item(2 * turn + 1, scores[1], scores[0], weights[1], True)
        return carry

    lax.fori_loop(0, count // 2 - 1, two, 0)
    item(count - 2, scores[0], scores[1], weights[0], True)
    item(count - 1, scores[1], scores[0], weights[1], False)


def prefill_kernel(info, queries, own, other, value_ref, out_ref, keys, bias, s0, s1, w0, w1):
    ctx, core = info[0], info[1]
    unpack(own, other, keys)
    key = lax.broadcasted_iota(jnp.int32, (TOKENS, POOL), 1)
    token = (key // BLOCK) * BLOCK + token_of_key((TOKENS, POOL), 1, core)
    query = ctx * TOKENS + lax.broadcasted_iota(jnp.int32, (TOKENS, POOL), 0)
    bias[...] = jnp.where(token <= query, 0.0, hidden)

    def emit(i, mixed):
        columns = pl.ds(pl.multiple_of(i * VALUE_DIM, VALUE_DIM), VALUE_DIM)
        out_ref[:, columns] = dot(mixed, value_ref[:, columns]).astype(jnp.bfloat16)

    attend(queries, keys, bias, (s0, s1), (w0, w1), emit)


def prefill(info, queries, own, other, absorb_values):
    return pl.pallas_call(
        prefill_kernel,
        out_shape=jax.ShapeDtypeStruct((TOKENS, HEADS * VALUE_DIM), jnp.bfloat16),
        in_specs=[smem] + [vmem] * 4,
        out_specs=vmem,
        scratch_shapes=[
            pltpu.VMEM((POOL, WIDTH), jnp.bfloat16),
            pltpu.VMEM((TOKENS, POOL), jnp.float32),
            pltpu.VMEM((TOKENS, POOL), jnp.float32),
            pltpu.VMEM((TOKENS, POOL), jnp.float32),
            pltpu.VMEM((TOKENS, POOL), jnp.bfloat16),
            pltpu.VMEM((TOKENS, POOL), jnp.bfloat16),
        ],
        compiler_params=params,
        cost_estimate=pl.CostEstimate(
            flops=2 * 2048 * 2048 * 1280, bytes_accessed=10_000_000, transcendentals=2048 * 2048
        ),
        name="prefill",
    )(info, queries, own, other, absorb_values)


def decode_kernel(
    info, queries, own, other, newest, bias, value_ref, weight_hbm,
    keep_ref, send_ref, keys, s0, s1, w0, w1, heads_out, weight, sem,
):
    core = info[1]
    load = pltpu.make_async_copy(weight_hbm, weight, sem)
    load.start()
    unpack(own, other, keys)
    keys[POOL:, :] = newest[...]

    def emit(i, mixed):
        for part in range(2):
            columns = pl.ds(pl.multiple_of((i * 2 + part) * VALUE_DIM, VALUE_DIM), VALUE_DIM)
            rows = mixed[part * QUERIES : (part + 1) * QUERIES]
            heads_out[:, columns] = dot(rows, value_ref[:, columns]).astype(jnp.bfloat16)

    attend(queries, keys, bias, (s0, s1), (w0, w1), emit)
    load.wait()

    def project(place, carry):
        columns = pl.ds(pl.multiple_of(place * 2 * SHARE, 2 * SHARE), 2 * SHARE)
        turned = dot(heads_out[...], weight[:, columns]).T
        first, second = turned[:SHARE], turned[SHARE:]
        keep_ref[place] = jnp.where(core == 0, first, second).astype(jnp.bfloat16)
        send_ref[place] = jnp.where(core == 0, second, first).astype(jnp.bfloat16)
        return carry

    lax.fori_loop(0, MODEL // (2 * SHARE), project, 0)


def decode(info, queries, own, other, newest, bias, absorb_values, out_weight):
    share = jax.ShapeDtypeStruct((8, SHARE, QUERIES), jnp.bfloat16)
    return pl.pallas_call(
        decode_kernel,
        out_shape=(share, share),
        in_specs=[smem] + [vmem] * 6 + [anywhere],
        out_specs=(vmem, vmem),
        scratch_shapes=[
            pltpu.VMEM((KEYS, WIDTH), jnp.bfloat16),
            pltpu.VMEM((2 * QUERIES, KEYS), jnp.float32),
            pltpu.VMEM((2 * QUERIES, KEYS), jnp.float32),
            pltpu.VMEM((2 * QUERIES, KEYS), jnp.bfloat16),
            pltpu.VMEM((2 * QUERIES, KEYS), jnp.bfloat16),
            pltpu.VMEM((QUERIES, HEADS * VALUE_DIM), jnp.bfloat16),
            pltpu.VMEM((HEADS * VALUE_DIM, MODEL), jnp.bfloat16),
            pltpu.SemaphoreType.DMA(()),
        ],
        compiler_params=params,
        cost_estimate=pl.CostEstimate(
            flops=2 * 1024 * 2176 * 1280 + 2 * 128 * 1024 * 7168,
            bytes_accessed=22_000_000,
            transcendentals=1024 * 2176,
        ),
        name="decode",
    )(info, queries, own, other, newest, bias, absorb_values, out_weight)


def gather_sum_kernel(parts, out_ref):
    total = parts[0].astype(jnp.float32)
    for place in range(1, parts.shape[0]):
        total = total + parts[place].astype(jnp.float32)
    out_ref[...] = total.T.astype(jnp.bfloat16)


def gather_sum(parts):
    return pl.pallas_call(
        gather_sum_kernel,
        out_shape=jax.ShapeDtypeStruct((QUERIES, SHARE), jnp.bfloat16),
        in_specs=[vmem],
        out_specs=vmem,
        name="gather_sum",
    )(parts)


def on_device(
    pre_queries,
    pre_latent,
    absorb_keys,
    absorb_values,
    step_queries,
    step_latent,
    context_lengths,
    page_table,
    out_weight,
):
    tp = lax.axis_index("tp")
    info = jnp.stack([lax.axis_index("ctx"), tp % 2]).astype(jnp.int32)
    own = lax.all_to_all(pack(pre_latent), BOTH, 0, 0, axis_index_groups=same_core_groups())
    ready = absorb(
        info,
        pre_queries,
        step_queries.reshape(QUERIES, HEADS * HEAD),
        absorb_keys,
        step_latent.reshape(QUERIES, LATENT + ROPE),
        context_lengths.reshape(ROWS, 1),
        page_table,
    )
    own, *ready = lax.optimization_barrier((own, *ready))
    pre_joined, step_joined, newest, bias = ready
    other = lax.ppermute(own, BOTH, other_core())
    keep, send = decode(
        info,
        step_joined.reshape(HEADS // 2, 2 * QUERIES, WIDTH),
        own,
        other,
        newest,
        bias,
        absorb_values,
        out_weight,
    )
    arrived = lax.ppermute(send, BOTH, other_core())
    chip = (keep.astype(jnp.float32) + arrived.astype(jnp.float32)).astype(jnp.bfloat16)
    chip, own, other = lax.optimization_barrier((chip, own, other))
    parts = lax.all_to_all(chip, BOTH, 0, 0, axis_index_groups=chip_groups())
    prefill_heads = prefill(info, pre_joined, own, other, absorb_values)
    decode_out = gather_sum(parts).reshape(STEPS, ROWS, SHARE)
    return (prefill_heads, decode_out)


def solution(mesh):
    return jax.shard_map(
        on_device,
        mesh=mesh,
        in_specs=(
            P("ctx", "tp"),
            P(("ctx", "tp"), None),
            P(None, "tp"),
            P(None, "tp"),
            P(None, "ctx", "tp"),
            P(None, "ctx", None),
            P("ctx"),
            P("ctx", None),
            P("tp", None),
        ),
        out_specs=(P("ctx", "tp"), P(None, "ctx", "tp")),
        check_vma=False,
    )
```

```python
import functools
import itertools
import math

import jax
import jax.numpy as jnp
from jax import lax
from jax.experimental import pallas as pl
from jax.experimental.pallas import tpu as pltpu
from jax.sharding import PartitionSpec as P

LATENT = 512
ROPE = 64
NOPE = 128
VALUE_DIM = 128
PAGE = 64
STEPS = 4
WIDTH = LATENT + 2 * ROPE
DIRECT = NOPE + 2 * ROPE
PIECE = 72
BLOCK = 256
HEAD = NOPE + ROPE
HEADS = 8
TOKENS = 256
ROWS = 32
QUERIES = STEPS * ROWS
POOL = 2048
KEYS = POOL + QUERIES
MODEL = 7168
SHARE = 448
BOTH = ("ctx", "tp")
NEWEST = HEADS * QUERIES
BIAS = NEWEST + QUERIES

hidden = -1e30
CUT = 1024
SOFT = 16
DECODE_CUT = 256
ATTEND_MIB = 52
to_exp2 = math.log2(math.e) / math.sqrt(HEAD)
vmem = pl.BlockSpec(memory_space=pltpu.VMEM)
smem = pl.BlockSpec(memory_space=pltpu.SMEM)
hbm = pl.BlockSpec(memory_space=pltpu.HBM)


def params(mib):
    return pltpu.CompilerParams(vmem_limit_bytes=mib * 1024 * 1024)


def flat(x, y, z, core):
    return (x * 2 + y // 2) * 16 + z * 4 + (y % 2) * 2 + core


def chips():
    return itertools.product(range(4), range(4), range(4), range(2))


def chip_groups():
    return [
        [flat(x, yh * 2 + yl, z, core) for z, yl in itertools.product(range(4), range(2))]
        for x, yh, core in itertools.product(range(4), range(2), range(2))
    ]


def other_core():
    return [(flat(x, y, z, c), flat(x, y, z, 1 - c)) for x, y, z, c in chips()]


def same_core_groups():
    return [
        [
            flat(x, yh * 2 + yl, z, core)
            for x, yh, z, yl in itertools.product(range(4), range(2), range(4), range(2))
        ]
        for core in range(2)
    ]


def dot(a, b):
    return jnp.dot(a, b, preferred_element_type=jnp.float32)


def dot_t(a, b):
    return lax.dot_general(a, b, (((1,), (1,)), ((), ())), preferred_element_type=jnp.float32)


def pack_kernel(latent_ref, out_ref):
    latent = latent_ref[...].astype(jnp.float32)
    rope = latent[:, LATENT:]
    parts = [latent[:, at : at + 128] for at in range(0, LATENT, 128)]
    parts.append(jnp.concatenate([rope[:8], rope[8:]], axis=1))
    piece = jnp.concatenate(parts, axis=0).astype(jnp.bfloat16)
    for place in range(64):
        out_ref[place] = piece


def pack(latent):
    return pl.pallas_call(
        pack_kernel,
        out_shape=jax.ShapeDtypeStruct((64, PIECE, 128), jnp.bfloat16),
        in_specs=[vmem],
        out_specs=vmem,
        name="pack",
    )(latent)


def unpack(own, other, latent, ropes):
    for block in range(POOL // BLOCK):
        for half, source in enumerate((own, other)):
            rows = slice(block * BLOCK + half * 128, block * BLOCK + half * 128 + 128)
            pieces = slice(block * 8, block * 8 + 8)
            for tile in range(4):
                latent[rows, tile * 128 : (tile + 1) * 128] = source[
                    pieces, tile * 16 : (tile + 1) * 16, :
                ].reshape(128, 128)
            rope = source[pieces, 64:72, :].astype(jnp.float32)
            left = lax.broadcasted_iota(jnp.int32, rope.shape, 2) < ROPE
            both = jnp.concatenate([jnp.where(left, rope, 0.0), jnp.where(left, 0.0, rope)], axis=1)
            both = both.reshape(128, 128).astype(jnp.bfloat16)
            for ref in ropes:
                ref[rows, ref.shape[1] - 2 * ROPE :] = both


def token_of_key(shape, dim, core):
    row = lax.broadcasted_iota(jnp.int32, shape, dim)
    owner = jnp.where((row // 128) % 2 == 0, core, 1 - core)
    return ((row % 128) // 16) * 32 + owner * 16 + row % 16


def absorb_kernel(info, query_ref, key_ref, latent_ref, length_ref, table_ref, out):
    core = info[1]
    for pair in range(HEADS // 2):
        both = query_ref[:, pair * 2 * HEAD : (pair + 1) * 2 * HEAD]
        for part in range(2):
            head = pair * 2 + part
            query = both[:, part * HEAD : (part + 1) * HEAD]
            key_map = key_ref[:, head * NOPE : (head + 1) * NOPE]
            rows = slice(head * QUERIES, (head + 1) * QUERIES)
            out[rows, :LATENT] = dot_t(query[:, :NOPE], key_map).astype(jnp.bfloat16)
            rope = query[:, NOPE:]
            out[rows, LATENT:] = jnp.concatenate([rope, rope], axis=1)
    rows = slice(NEWEST, NEWEST + QUERIES)
    out[rows, : LATENT + ROPE] = latent_ref[...]
    out[rows, LATENT + ROPE :] = jnp.zeros((QUERIES, ROPE), jnp.bfloat16)
    table = table_ref[...]
    pages = table.shape[1]
    page = lax.broadcasted_iota(jnp.int32, table.shape, 1)
    slot = jnp.zeros(table.shape, jnp.int32)
    for place in range(pages):
        slot = slot + jnp.where(table[:, place : place + 1] == page, place, 0)
    limit = jnp.clip(length_ref[...] - slot * PAGE, 0, PAGE).astype(jnp.float32)
    shape = (pages, POOL)
    key = lax.broadcasted_iota(jnp.int32, shape, 1)
    of = (key // BLOCK) * (BLOCK // PAGE) + (key % 128) // (PAGE // 2)
    owner = (lax.broadcasted_iota(jnp.int32, shape, 0) == of).astype(jnp.bfloat16)
    spread = dot(limit.astype(jnp.bfloat16), owner)
    token = (token_of_key((ROWS, POOL), 1, core) % PAGE).astype(jnp.float32)
    pool = jnp.where(token < spread, 0.0, hidden)
    mine = lax.broadcasted_iota(jnp.int32, (QUERIES, QUERIES), 0)
    theirs = lax.broadcasted_iota(jnp.int32, (QUERIES, QUERIES), 1)
    seen = (mine % ROWS == theirs % ROWS) & (theirs // ROWS <= mine // ROWS)
    bias = jnp.concatenate([pool] * STEPS, axis=0)
    bias = jnp.concatenate([bias, jnp.where(seen, 0.0, hidden)], axis=1).astype(jnp.bfloat16)
    for at in range(0, KEYS, WIDTH):
        part = bias[:, at : at + WIDTH]
        row = BIAS + at // WIDTH * QUERIES
        out[row : row + QUERIES, : part.shape[1]] = part


def absorb(info, queries, absorb_keys, step_latent, lengths, table):
    return pl.pallas_call(
        absorb_kernel,
        out_shape=jax.ShapeDtypeStruct((BIAS + 4 * QUERIES, WIDTH), jnp.bfloat16),
        in_specs=[smem] + [vmem] * 5,
        out_specs=vmem,
        compiler_params=params(56),
        cost_estimate=pl.CostEstimate(
            flops=2 * 1024 * 128 * 512, bytes_accessed=5_000_000, transcendentals=0
        ),
        name="absorb",
    )(info, queries, absorb_keys, step_latent, lengths, table)


def softmax_rows(scores, bias, weights, start, count):
    bias_start = start % bias.shape[0]
    shifted = scores[start : start + count, :] + bias[bias_start : bias_start + count, :]
    largest = jnp.max(shifted, axis=1, keepdims=True)
    expo = jnp.exp2(shifted * to_exp2 - largest * to_exp2)
    weights[start : start + count, :] = expo.astype(jnp.bfloat16)
    return 1.0 / jnp.sum(expo, axis=1, keepdims=True)


def prefill_kernel(
    info, own, other, query_ref, key_map, value_map, out_ref, queries, latent, bias, *held
):
    ctx, core = info[0], info[1]
    keys, values, scores, weights = held[:2], held[2:6], held[6:8], held[8:]
    unpack(own, other, latent, keys)
    for pair in range(HEADS // 2):
        both = query_ref[:, pair * 2 * HEAD : (pair + 1) * 2 * HEAD]
        for part in range(2):
            query = both[:, part * HEAD : (part + 1) * HEAD]
            rope = query[:, NOPE:]
            queries[pair * 2 + part] = jnp.concatenate([query[:, :NOPE], rope, rope], axis=1)
    key = lax.broadcasted_iota(jnp.int32, (TOKENS, POOL), 1)
    token = (key // BLOCK) * BLOCK + token_of_key((TOKENS, POOL), 1, core)
    query = ctx * TOKENS + lax.broadcasted_iota(jnp.int32, (TOKENS, POOL), 0)
    bias[...] = jnp.where(token <= query, 0.0, hidden)
    inverse = {}

    def make(head, at):
        columns = slice(head * NOPE, (head + 1) * NOPE)
        maps = jnp.concatenate([key_map[:, columns], value_map[:, columns]], axis=1)
        made = dot(latent[at : at + CUT, :], maps).astype(jnp.bfloat16)
        keys[head % 2][at : at + CUT, :NOPE] = made[:, :NOPE]
        values[head % 4][at : at + CUT, :] = made[:, NOPE:]

    def score(head, at):
        scores[head % 2][:, at : at + CUT] = dot_t(queries[head], keys[head % 2][at : at + CUT, :])

    def soften(head, start):
        part = softmax_rows(scores[head % 2], bias, weights[head % 2], start, SOFT)
        inverse.setdefault(head, []).append(part)

    def mix(head):
        mixed = dot(weights[head % 2][...], values[head % 4][...])
        scaled = mixed * jnp.concatenate(inverse[head], axis=0)
        out_ref[:, head * VALUE_DIM : (head + 1) * VALUE_DIM] = scaled.astype(jnp.bfloat16)

    turns = TOKENS // SOFT
    cuts = POOL // CUT
    for stage in range(HEADS + 3):
        if 0 <= stage - 3 < HEADS:
            mix(stage - 3)
        for turn in range(turns):
            for cut in range(turn * cuts // turns, (turn + 1) * cuts // turns):
                if 0 <= stage - 1 < HEADS:
                    score(stage - 1, cut * CUT)
                if stage < HEADS:
                    make(stage, cut * CUT)
            if 0 <= stage - 2 < HEADS:
                soften(stage - 2, turn * SOFT)


def prefill(info, own, other, queries, absorb_keys, absorb_values):
    return pl.pallas_call(
        prefill_kernel,
        out_shape=jax.ShapeDtypeStruct((TOKENS, HEADS * VALUE_DIM), jnp.bfloat16),
        in_specs=[smem] + [vmem] * 5,
        out_specs=vmem,
        scratch_shapes=[
            pltpu.VMEM((HEADS, TOKENS, DIRECT), jnp.bfloat16),
            pltpu.VMEM((POOL, LATENT), jnp.bfloat16),
            pltpu.VMEM((TOKENS, POOL), jnp.float32),
            *[pltpu.VMEM((POOL, DIRECT), jnp.bfloat16)] * 2,
            *[pltpu.VMEM((POOL, VALUE_DIM), jnp.bfloat16)] * 4,
            *[pltpu.VMEM((TOKENS, POOL), jnp.float32)] * 2,
            *[pltpu.VMEM((TOKENS, POOL), jnp.bfloat16)] * 2,
        ],
        compiler_params=params(ATTEND_MIB),
        cost_estimate=pl.CostEstimate(
            flops=2 * 2048 * 2048 * 1024, bytes_accessed=10_000_000, transcendentals=2048 * 2048
        ),
        name="prefill",
    )(info, own, other, queries, absorb_keys, absorb_values)


def decode_kernel(
    info, own, other, ready, value_ref, weight_hbm,
    keep_ref, send_ref, weight, sem, keys, bias, s0, s1, w0, w1, heads_out,
):
    core = info[1]
    load = pltpu.make_async_copy(weight_hbm, weight, sem)
    load.start()
    unpack(own, other, keys, [keys])
    keys[POOL:, :] = ready[NEWEST:BIAS, :]
    for at in range(0, KEYS, WIDTH):
        row = BIAS + at // WIDTH * QUERIES
        size = min(WIDTH, KEYS - at)
        bias[:, at : at + size] = ready[row : row + QUERIES, :size].astype(jnp.float32)
    scores, weights = (s0, s1), (w0, w1)
    inverse = {}
    items = HEADS // 2
    rows = 2 * QUERIES

    def score(item, at, size):
        queries = ready[item * rows : (item + 1) * rows, :]
        scores[item % 2][:, at : at + size] = dot_t(queries, keys[at : at + size, :])

    def soften(item, start):
        part = softmax_rows(scores[item % 2], bias, weights[item % 2], start, SOFT)
        inverse.setdefault(item, []).append(part)

    def mix(item):
        scale = jnp.concatenate(inverse[item], axis=0)
        mixed = [
            (dot(weights[item % 2][...], keys[:, at : at + 256]) * scale).astype(jnp.bfloat16)
            for at in range(0, LATENT, 256)
        ]
        mixed = jnp.concatenate(mixed, axis=1)
        for part in range(2):
            head = item * 2 + part
            columns = slice(head * VALUE_DIM, (head + 1) * VALUE_DIM)
            heads_out[:, columns] = dot(
                mixed[part * QUERIES : (part + 1) * QUERIES], value_ref[:, columns]
            ).astype(jnp.bfloat16)

    turns = rows // SOFT
    parts = [(at, min(DECODE_CUT, KEYS - at)) for at in range(0, KEYS, DECODE_CUT)]
    for stage in range(items + 2):
        if 0 <= stage - 2 < items:
            mix(stage - 2)
        for turn in range(turns):
            if stage < items:
                for at, size in parts[turn * len(parts) // turns : (turn + 1) * len(parts) // turns]:
                    score(stage, at, size)
            if 0 <= stage - 1 < items:
                soften(stage - 1, turn * SOFT)
    load.wait()

    for place in range(8):
        columns = slice(place * 2 * SHARE, (place + 1) * 2 * SHARE)
        turned = dot(heads_out[...], weight[:, columns]).T
        first, second = turned[:SHARE], turned[SHARE:]
        keep_ref[place] = jnp.where(core == 0, first, second).astype(jnp.bfloat16)
        send_ref[place] = jnp.where(core == 0, second, first).astype(jnp.bfloat16)


def decode(info, own, other, ready, absorb_values, out_weight):
    share = jax.ShapeDtypeStruct((8, SHARE, QUERIES), jnp.bfloat16)
    return pl.pallas_call(
        decode_kernel,
        out_shape=(share, share),
        in_specs=[smem] + [vmem] * 4 + [hbm],
        out_specs=(vmem, vmem),
        scratch_shapes=[
            pltpu.VMEM((HEADS * VALUE_DIM, MODEL), jnp.bfloat16),
            pltpu.SemaphoreType.DMA(()),
            pltpu.VMEM((KEYS, WIDTH), jnp.bfloat16),
            pltpu.VMEM((QUERIES, KEYS), jnp.float32),
            pltpu.VMEM((2 * QUERIES, KEYS), jnp.float32),
            pltpu.VMEM((2 * QUERIES, KEYS), jnp.float32),
            pltpu.VMEM((2 * QUERIES, KEYS), jnp.bfloat16),
            pltpu.VMEM((2 * QUERIES, KEYS), jnp.bfloat16),
            pltpu.VMEM((QUERIES, HEADS * VALUE_DIM), jnp.bfloat16),
        ],
        compiler_params=params(ATTEND_MIB),
        cost_estimate=pl.CostEstimate(
            flops=2 * 1024 * 2176 * 1280 + 2 * 128 * 1024 * 7168,
            bytes_accessed=22_000_000,
            transcendentals=1024 * 2176,
        ),
        name="decode",
    )(info, own, other, ready, absorb_values, out_weight)


def gather_sum_kernel(parts, out_ref):
    total = parts[0].astype(jnp.float32)
    for place in range(1, parts.shape[0]):
        total = total + parts[place].astype(jnp.float32)
    out_ref[...] = total.T.astype(jnp.bfloat16)


def gather_sum(parts):
    return pl.pallas_call(
        gather_sum_kernel,
        out_shape=jax.ShapeDtypeStruct((QUERIES, SHARE), jnp.bfloat16),
        in_specs=[vmem],
        out_specs=vmem,
        name="gather_sum",
    )(parts)


def on_device(
    pre_queries,
    pre_latent,
    absorb_keys,
    absorb_values,
    step_queries,
    step_latent,
    context_lengths,
    page_table,
    out_weight,
):
    tp = lax.axis_index("tp")
    info = jnp.stack([lax.axis_index("ctx"), tp % 2]).astype(jnp.int32)
    own = lax.all_to_all(pack(pre_latent), BOTH, 0, 0, axis_index_groups=same_core_groups())
    ready = absorb(
        info,
        step_queries.reshape(QUERIES, HEADS * HEAD),
        absorb_keys,
        step_latent.reshape(QUERIES, LATENT + ROPE),
        context_lengths.reshape(ROWS, 1),
        page_table,
    )
    own, ready = lax.optimization_barrier((own, ready))
    other = lax.ppermute(own, BOTH, other_core())
    keep, send = decode(info, own, other, ready, absorb_values, out_weight)
    arrived = lax.ppermute(send, BOTH, other_core())
    chip = (keep.astype(jnp.float32) + arrived.astype(jnp.float32)).astype(jnp.bfloat16)
    chip, own, other = lax.optimization_barrier((chip, own, other))
    parts = lax.all_to_all(chip, BOTH, 0, 0, axis_index_groups=chip_groups())
    prefill_heads = prefill(info, own, other, pre_queries, absorb_keys, absorb_values)
    decode_out = gather_sum(parts).reshape(STEPS, ROWS, SHARE)
    return (prefill_heads, decode_out)


def solution(mesh):
    return jax.shard_map(
        on_device,
        mesh=mesh,
        in_specs=(
            P("ctx", "tp"),
            P(("ctx", "tp"), None),
            P(None, "tp"),
            P(None, "tp"),
            P(None, "ctx", "tp"),
            P(None, "ctx", None),
            P("ctx"),
            P("ctx", None),
            P("tp", None),
        ),
        out_specs=(P("ctx", "tp"), P(None, "ctx", "tp")),
        check_vma=False,
    )
```

```python
import functools
import itertools
import math

import jax
import jax.numpy as jnp
from jax import lax
from jax.experimental import pallas as pl
from jax.experimental.pallas import tpu as pltpu
from jax.sharding import PartitionSpec as P

LATENT = 512
ROPE = 64
NOPE = 128
VALUE_DIM = 128
PAGE = 64
STEPS = 4
WIDTH = LATENT + 2 * ROPE
DIRECT = NOPE + 2 * ROPE
PIECE = 72
BLOCK = 256
HEAD = NOPE + ROPE
HEADS = 8
TOKENS = 256
ROWS = 32
QUERIES = STEPS * ROWS
POOL = 2048
KEYS = POOL + QUERIES
MODEL = 7168
SHARE = 448
BOTH = ("ctx", "tp")
NEWEST = HEADS * QUERIES
BIAS = NEWEST + QUERIES

hidden = -1e30
CUT = 1024
SOFT = 16
DECODE_CUT = 256
PREFILL_MIB = 48
DECODE_MIB = 48
to_exp2 = math.log2(math.e) / math.sqrt(HEAD)
vmem = pl.BlockSpec(memory_space=pltpu.VMEM)
smem = pl.BlockSpec(memory_space=pltpu.SMEM)
hbm = pl.BlockSpec(memory_space=pltpu.HBM)


def params(mib):
    return pltpu.CompilerParams(vmem_limit_bytes=mib * 1024 * 1024)


def flat(x, y, z, core):
    return (x * 2 + y // 2) * 16 + z * 4 + (y % 2) * 2 + core


def chips():
    return itertools.product(range(4), range(4), range(4), range(2))


def chip_groups():
    return [
        [flat(x, yh * 2 + yl, z, core) for z, yl in itertools.product(range(4), range(2))]
        for x, yh, core in itertools.product(range(4), range(2), range(2))
    ]


def other_core():
    return [(flat(x, y, z, c), flat(x, y, z, 1 - c)) for x, y, z, c in chips()]


def same_core_groups():
    return [
        [
            flat(x, yh * 2 + yl, z, core)
            for x, yh, z, yl in itertools.product(range(4), range(2), range(4), range(2))
        ]
        for core in range(2)
    ]


def dot(a, b):
    return jnp.dot(a, b, preferred_element_type=jnp.float32)


def dot_t(a, b):
    return lax.dot_general(a, b, (((1,), (1,)), ((), ())), preferred_element_type=jnp.float32)


def pack_kernel(latent_ref, out_ref):
    latent = latent_ref[...].astype(jnp.float32)
    rope = latent[:, LATENT:]
    parts = [latent[:, at : at + 128] for at in range(0, LATENT, 128)]
    parts.append(jnp.concatenate([rope[:8], rope[8:]], axis=1))
    piece = jnp.concatenate(parts, axis=0).astype(jnp.bfloat16)
    for place in range(64):
        out_ref[place] = piece


def pack(latent):
    return pl.pallas_call(
        pack_kernel,
        out_shape=jax.ShapeDtypeStruct((64, PIECE, 128), jnp.bfloat16),
        in_specs=[vmem],
        out_specs=vmem,
        compiler_params=params(16),
        name="pack",
    )(latent)


def unpack(own, other, latent, ropes):
    for block in range(POOL // BLOCK):
        for half, source in enumerate((own, other)):
            rows = slice(block * BLOCK + half * 128, block * BLOCK + half * 128 + 128)
            pieces = slice(block * 8, block * 8 + 8)
            for tile in range(4):
                latent[rows, tile * 128 : (tile + 1) * 128] = source[
                    pieces, tile * 16 : (tile + 1) * 16, :
                ].reshape(128, 128)
            rope = source[pieces, 64:72, :].astype(jnp.float32)
            left = lax.broadcasted_iota(jnp.int32, rope.shape, 2) < ROPE
            both = jnp.concatenate([jnp.where(left, rope, 0.0), jnp.where(left, 0.0, rope)], axis=1)
            both = both.reshape(128, 128).astype(jnp.bfloat16)
            for ref in ropes:
                ref[rows, ref.shape[1] - 2 * ROPE :] = both


def token_of_key(shape, dim, core):
    row = lax.broadcasted_iota(jnp.int32, shape, dim)
    owner = jnp.where((row // 128) % 2 == 0, core, 1 - core)
    return ((row % 128) // 16) * 32 + owner * 16 + row % 16


def place_of_head(head):
    row = 2 * LATENT + head // 4 * TOKENS
    return slice(row, row + TOKENS), slice(head % 4 * DIRECT, (head % 4 + 1) * DIRECT)


def absorb_kernel(
    info, query_ref, key_ref, latent_ref, length_ref, table_ref, pre_ref, value_ref, out, pre_out
):
    core = info[1]
    pre_out[:LATENT, :] = key_ref[...]
    pre_out[LATENT : 2 * LATENT, :] = value_ref[...]
    for head in range(HEADS):
        query = pre_ref[:, head // 2 * 2 * HEAD : (head // 2 + 1) * 2 * HEAD]
        query = query[:, head % 2 * HEAD : (head % 2 + 1) * HEAD]
        rope = query[:, NOPE:]
        rows, columns = place_of_head(head)
        pre_out[rows, columns] = jnp.concatenate([query[:, :NOPE], rope, rope], axis=1)
    for pair in range(HEADS // 2):
        both = query_ref[:, pair * 2 * HEAD : (pair + 1) * 2 * HEAD]
        for part in range(2):
            head = pair * 2 + part
            query = both[:, part * HEAD : (part + 1) * HEAD]
            key_map = key_ref[:, head * NOPE : (head + 1) * NOPE]
            rows = slice(head * QUERIES, (head + 1) * QUERIES)
            out[rows, :LATENT] = dot_t(query[:, :NOPE], key_map).astype(jnp.bfloat16)
            rope = query[:, NOPE:]
            out[rows, LATENT:] = jnp.concatenate([rope, rope], axis=1)
    rows = slice(NEWEST, NEWEST + QUERIES)
    out[rows, : LATENT + ROPE] = latent_ref[...]
    out[rows, LATENT + ROPE :] = jnp.zeros((QUERIES, ROPE), jnp.bfloat16)
    table = table_ref[...]
    pages = table.shape[1]
    page = lax.broadcasted_iota(jnp.int32, table.shape, 1)
    slot = jnp.zeros(table.shape, jnp.int32)
    for place in range(pages):
        slot = slot + jnp.where(table[:, place : place + 1] == page, place, 0)
    limit = jnp.clip(length_ref[...] - slot * PAGE, 0, PAGE).astype(jnp.float32)
    shape = (pages, POOL)
    key = lax.broadcasted_iota(jnp.int32, shape, 1)
    of = (key // BLOCK) * (BLOCK // PAGE) + (key % 128) // (PAGE // 2)
    owner = (lax.broadcasted_iota(jnp.int32, shape, 0) == of).astype(jnp.bfloat16)
    spread = dot(limit.astype(jnp.bfloat16), owner)
    token = (token_of_key((ROWS, POOL), 1, core) % PAGE).astype(jnp.float32)
    pool = jnp.where(token < spread, 0.0, hidden)
    mine = lax.broadcasted_iota(jnp.int32, (QUERIES, QUERIES), 0)
    theirs = lax.broadcasted_iota(jnp.int32, (QUERIES, QUERIES), 1)
    seen = (mine % ROWS == theirs % ROWS) & (theirs // ROWS <= mine // ROWS)
    bias = jnp.concatenate([pool] * STEPS, axis=0)
    bias = jnp.concatenate([bias, jnp.where(seen, 0.0, hidden)], axis=1).astype(jnp.bfloat16)
    for at in range(0, KEYS, WIDTH):
        part = bias[:, at : at + WIDTH]
        row = BIAS + at // WIDTH * QUERIES
        out[row : row + QUERIES, : part.shape[1]] = part


def absorb(info, queries, absorb_keys, step_latent, lengths, table, pre_queries, absorb_values):
    return pl.pallas_call(
        absorb_kernel,
        out_shape=(
            jax.ShapeDtypeStruct((BIAS + 4 * QUERIES, WIDTH), jnp.bfloat16),
            jax.ShapeDtypeStruct((2 * LATENT + 2 * TOKENS, HEADS * NOPE), jnp.bfloat16),
        ),
        in_specs=[smem] + [vmem] * 7,
        out_specs=(vmem, vmem),
        compiler_params=params(56),
        cost_estimate=pl.CostEstimate(
            flops=2 * 1024 * 128 * 512, bytes_accessed=5_000_000, transcendentals=0
        ),
        name="absorb",
    )(info, queries, absorb_keys, step_latent, lengths, table, pre_queries, absorb_values)


def softmax_rows(scores, bias, weights, start, count):
    bias_start = start % bias.shape[0]
    shifted = scores[start : start + count, :] + bias[bias_start : bias_start + count, :]
    largest = jnp.max(shifted, axis=1, keepdims=True)
    expo = jnp.exp2(shifted * to_exp2 - largest * to_exp2)
    weights[start : start + count, :] = expo.astype(jnp.bfloat16)
    return 1.0 / jnp.sum(expo, axis=1, keepdims=True)


def prefill_kernel(info, own, other, ready, out_ref, latent, bias, *held):
    ctx, core = info[0], info[1]
    keys, values, scores, weights = held[:2], held[2:6], held[6:8], held[8:]
    unpack(own, other, latent, keys)
    key = lax.broadcasted_iota(jnp.int32, (TOKENS, POOL), 1)
    token = (key // BLOCK) * BLOCK + token_of_key((TOKENS, POOL), 1, core)
    query = ctx * TOKENS + lax.broadcasted_iota(jnp.int32, (TOKENS, POOL), 0)
    bias[...] = jnp.where(token <= query, 0.0, hidden)
    inverse = {}

    def make(head, at):
        columns = slice(head * NOPE, (head + 1) * NOPE)
        maps = [ready[:LATENT, columns], ready[LATENT : 2 * LATENT, columns]]
        maps = jnp.concatenate(maps, axis=1)
        made = dot(latent[at : at + CUT, :], maps).astype(jnp.bfloat16)
        keys[head % 2][at : at + CUT, :NOPE] = made[:, :NOPE]
        values[head % 4][at : at + CUT, :] = made[:, NOPE:]

    def score(head, at):
        query = ready[place_of_head(head)]
        scores[head % 2][:, at : at + CUT] = dot_t(query, keys[head % 2][at : at + CUT, :])

    def soften(head, start):
        part = softmax_rows(scores[head % 2], bias, weights[head % 2], start, SOFT)
        inverse.setdefault(head, []).append(part)

    def mix(head):
        mixed = dot(weights[head % 2][...], values[head % 4][...])
        scaled = mixed * jnp.concatenate(inverse[head], axis=0)
        out_ref[:, head * VALUE_DIM : (head + 1) * VALUE_DIM] = scaled.astype(jnp.bfloat16)

    turns = TOKENS // SOFT
    cuts = POOL // CUT
    for stage in range(HEADS + 3):
        if 0 <= stage - 3 < HEADS:
            mix(stage - 3)
        for turn in range(turns):
            for cut in range(turn * cuts // turns, (turn + 1) * cuts // turns):
                if 0 <= stage - 1 < HEADS:
                    score(stage - 1, cut * CUT)
                if stage < HEADS:
                    make(stage, cut * CUT)
            if 0 <= stage - 2 < HEADS:
                soften(stage - 2, turn * SOFT)


def prefill(info, own, other, ready):
    return pl.pallas_call(
        prefill_kernel,
        out_shape=jax.ShapeDtypeStruct((TOKENS, HEADS * VALUE_DIM), jnp.bfloat16),
        in_specs=[smem] + [vmem] * 3,
        out_specs=vmem,
        scratch_shapes=[
            pltpu.VMEM((POOL, LATENT), jnp.bfloat16),
            pltpu.VMEM((TOKENS, POOL), jnp.float32),
            *[pltpu.VMEM((POOL, DIRECT), jnp.bfloat16)] * 2,
            *[pltpu.VMEM((POOL, VALUE_DIM), jnp.bfloat16)] * 4,
            *[pltpu.VMEM((TOKENS, POOL), jnp.float32)] * 2,
            *[pltpu.VMEM((TOKENS, POOL), jnp.bfloat16)] * 2,
        ],
        compiler_params=params(PREFILL_MIB),
        cost_estimate=pl.CostEstimate(
            flops=2 * 2048 * 2048 * 1024, bytes_accessed=10_000_000, transcendentals=2048 * 2048
        ),
        name="prefill",
    )(info, own, other, ready)


def decode_kernel(
    info, own, other, ready, value_ref, weight_hbm,
    keep_ref, send_ref, weight, sem, keys, bias, s0, s1, w0, w1, heads_out,
):
    core = info[1]
    load = pltpu.make_async_copy(weight_hbm, weight, sem)
    load.start()
    unpack(own, other, keys, [keys])
    keys[POOL:, :] = ready[NEWEST:BIAS, :]
    for at in range(0, KEYS, WIDTH):
        row = BIAS + at // WIDTH * QUERIES
        size = min(WIDTH, KEYS - at)
        bias[:, at : at + size] = ready[row : row + QUERIES, :size].astype(jnp.float32)
    scores, weights = (s0, s1), (w0, w1)
    inverse = {}
    items = HEADS // 2
    rows = 2 * QUERIES

    def score(item, at, size):
        queries = ready[item * rows : (item + 1) * rows, :]
        scores[item % 2][:, at : at + size] = dot_t(queries, keys[at : at + size, :])

    def soften(item, start):
        part = softmax_rows(scores[item % 2], bias, weights[item % 2], start, SOFT)
        inverse.setdefault(item, []).append(part)

    def mix(item):
        scale = jnp.concatenate(inverse[item], axis=0)
        mixed = [
            (dot(weights[item % 2][...], keys[:, at : at + 256]) * scale).astype(jnp.bfloat16)
            for at in range(0, LATENT, 256)
        ]
        mixed = jnp.concatenate(mixed, axis=1)
        for part in range(2):
            head = item * 2 + part
            columns = slice(head * VALUE_DIM, (head + 1) * VALUE_DIM)
            heads_out[:, columns] = dot(
                mixed[part * QUERIES : (part + 1) * QUERIES], value_ref[:, columns]
            ).astype(jnp.bfloat16)

    turns = rows // SOFT
    parts = [(at, min(DECODE_CUT, KEYS - at)) for at in range(0, KEYS, DECODE_CUT)]
    for stage in range(items + 2):
        if 0 <= stage - 2 < items:
            mix(stage - 2)
        for turn in range(turns):
            if stage < items:
                for at, size in parts[turn * len(parts) // turns : (turn + 1) * len(parts) // turns]:
                    score(stage, at, size)
            if 0 <= stage - 1 < items:
                soften(stage - 1, turn * SOFT)
    load.wait()

    for place in range(8):
        columns = slice(place * 2 * SHARE, (place + 1) * 2 * SHARE)
        turned = dot(heads_out[...], weight[:, columns]).T
        first, second = turned[:SHARE], turned[SHARE:]
        keep_ref[place] = jnp.where(core == 0, first, second).astype(jnp.bfloat16)
        send_ref[place] = jnp.where(core == 0, second, first).astype(jnp.bfloat16)


def decode(info, own, other, ready, absorb_values, out_weight):
    share = jax.ShapeDtypeStruct((8, SHARE, QUERIES), jnp.bfloat16)
    return pl.pallas_call(
        decode_kernel,
        out_shape=(share, share),
        in_specs=[smem] + [vmem] * 4 + [hbm],
        out_specs=(vmem, vmem),
        scratch_shapes=[
            pltpu.VMEM((HEADS * VALUE_DIM, MODEL), jnp.bfloat16),
            pltpu.SemaphoreType.DMA(()),
            pltpu.VMEM((KEYS, WIDTH), jnp.bfloat16),
            pltpu.VMEM((QUERIES, KEYS), jnp.float32),
            pltpu.VMEM((2 * QUERIES, KEYS), jnp.float32),
            pltpu.VMEM((2 * QUERIES, KEYS), jnp.float32),
            pltpu.VMEM((2 * QUERIES, KEYS), jnp.bfloat16),
            pltpu.VMEM((2 * QUERIES, KEYS), jnp.bfloat16),
            pltpu.VMEM((QUERIES, HEADS * VALUE_DIM), jnp.bfloat16),
        ],
        compiler_params=params(DECODE_MIB),
        cost_estimate=pl.CostEstimate(
            flops=2 * 1024 * 2176 * 1280 + 2 * 128 * 1024 * 7168,
            bytes_accessed=22_000_000,
            transcendentals=1024 * 2176,
        ),
        name="decode",
    )(info, own, other, ready, absorb_values, out_weight)


def gather_sum_kernel(parts, out_ref):
    total = parts[0].astype(jnp.float32)
    for place in range(1, parts.shape[0]):
        total = total + parts[place].astype(jnp.float32)
    out_ref[...] = total.T.astype(jnp.bfloat16)


def gather_sum(parts):
    return pl.pallas_call(
        gather_sum_kernel,
        out_shape=jax.ShapeDtypeStruct((QUERIES, SHARE), jnp.bfloat16),
        in_specs=[vmem],
        out_specs=vmem,
        compiler_params=params(16),
        name="gather_sum",
    )(parts)


def on_device(
    pre_queries,
    pre_latent,
    absorb_keys,
    absorb_values,
    step_queries,
    step_latent,
    context_lengths,
    page_table,
    out_weight,
):
    tp = lax.axis_index("tp")
    info = jnp.stack([lax.axis_index("ctx"), tp % 2]).astype(jnp.int32)
    own = lax.all_to_all(pack(pre_latent), BOTH, 0, 0, axis_index_groups=same_core_groups())
    ready, pre_ready = absorb(
        info,
        step_queries.reshape(QUERIES, HEADS * HEAD),
        absorb_keys,
        step_latent.reshape(QUERIES, LATENT + ROPE),
        context_lengths.reshape(ROWS, 1),
        page_table,
        pre_queries,
        absorb_values,
    )
    own, ready, pre_ready = lax.optimization_barrier((own, ready, pre_ready))
    other = lax.ppermute(own, BOTH, other_core())
    keep, send = decode(info, own, other, ready, absorb_values, out_weight)
    arrived = lax.ppermute(send, BOTH, other_core())
    chip = (keep.astype(jnp.float32) + arrived.astype(jnp.float32)).astype(jnp.bfloat16)
    chip, own, other = lax.optimization_barrier((chip, own, other))
    parts = lax.all_to_all(chip, BOTH, 0, 0, axis_index_groups=chip_groups())
    prefill_heads = prefill(info, own, other, pre_ready)
    decode_out = gather_sum(parts).reshape(STEPS, ROWS, SHARE)
    return (prefill_heads, decode_out)


def solution(mesh):
    return jax.shard_map(
        on_device,
        mesh=mesh,
        in_specs=(
            P("ctx", "tp"),
            P(("ctx", "tp"), None),
            P(None, "tp"),
            P(None, "tp"),
            P(None, "ctx", "tp"),
            P(None, "ctx", None),
            P("ctx"),
            P("ctx", None),
            P("tp", None),
        ),
        out_specs=(P("ctx", "tp"), P(None, "ctx", "tp")),
        check_vma=False,
    )
```

```python
import functools
import itertools
import math

import jax
import jax.numpy as jnp
from jax import lax
from jax.experimental import pallas as pl
from jax.experimental.pallas import tpu as pltpu
from jax.sharding import PartitionSpec as P

LATENT = 512
ROPE = 64
NOPE = 128
VALUE_DIM = 128
PAGE = 64
STEPS = 4
WIDTH = LATENT + 2 * ROPE
DIRECT = NOPE + 2 * ROPE
PIECE = 72
HALF = 1024
HEAD = NOPE + ROPE
HEADS = 8
TOKENS = 256
ROWS = 32
QUERIES = STEPS * ROWS
POOL = 2048
KEYS = POOL + QUERIES
MODEL = 7168
SHARE = 448
BOTH = ("ctx", "tp")
NEWEST = HEADS * QUERIES
BIAS = NEWEST + QUERIES

hidden = -1e30
CUT = 1024
SOFT = 16
DECODE_CUT = 256
PREFILL_MIB = 48
DECODE_MIB = 34
EARLY_MIB = 43
EARLY = 256
to_exp2 = math.log2(math.e) / math.sqrt(HEAD)
vmem = pl.BlockSpec(memory_space=pltpu.VMEM)
smem = pl.BlockSpec(memory_space=pltpu.SMEM)
hbm = pl.BlockSpec(memory_space=pltpu.HBM)


def params(mib):
    return pltpu.CompilerParams(vmem_limit_bytes=mib * 1024 * 1024)


def flat(x, y, z, core):
    return (x * 2 + y // 2) * 16 + z * 4 + (y % 2) * 2 + core


def chips():
    return itertools.product(range(4), range(4), range(4), range(2))


def chip_groups():
    return [
        [flat(x, yh * 2 + yl, z, core) for z, yl in itertools.product(range(4), range(2))]
        for x, yh, core in itertools.product(range(4), range(2), range(2))
    ]


def other_core():
    return [(flat(x, y, z, c), flat(x, y, z, 1 - c)) for x, y, z, c in chips()]


def same_core_groups():
    return [
        [
            flat(x, yh * 2 + yl, z, core)
            for x, yh, z, yl in itertools.product(range(4), range(2), range(4), range(2))
        ]
        for core in range(2)
    ]


def dot(a, b):
    return jnp.dot(a, b, preferred_element_type=jnp.float32)


def dot_t(a, b):
    return lax.dot_general(a, b, (((1,), (1,)), ((), ())), preferred_element_type=jnp.float32)


def pack_kernel(latent_ref, out_ref):
    latent = latent_ref[...].astype(jnp.float32)
    rope = latent[:, LATENT:]
    parts = [latent[:, at : at + 128] for at in range(0, LATENT, 128)]
    parts.append(jnp.concatenate([rope[:8], rope[8:]], axis=1))
    piece = jnp.concatenate(parts, axis=0).astype(jnp.bfloat16)
    for place in range(64):
        out_ref[place] = piece


def pack(latent):
    return pl.pallas_call(
        pack_kernel,
        out_shape=jax.ShapeDtypeStruct((64, PIECE, 128), jnp.bfloat16),
        in_specs=[vmem],
        out_specs=vmem,
        compiler_params=params(16),
        name="pack",
    )(latent)


def unpack(source, latent, ropes, at):
    for piece in range(0, 64, 8):
        rows = slice(at + piece * 16, at + piece * 16 + 128)
        pieces = slice(piece, piece + 8)
        for tile in range(4):
            latent[rows, tile * 128 : (tile + 1) * 128] = source[
                pieces, tile * 16 : (tile + 1) * 16, :
            ].reshape(128, 128)
        rope = source[pieces, 64:72, :].astype(jnp.float32)
        left = lax.broadcasted_iota(jnp.int32, rope.shape, 2) < ROPE
        both = jnp.concatenate([jnp.where(left, rope, 0.0), jnp.where(left, 0.0, rope)], axis=1)
        both = both.reshape(128, 128).astype(jnp.bfloat16)
        for ref in ropes:
            ref[rows, ref.shape[1] - 2 * ROPE :] = both


def token_of_key(shape, dim, core):
    key = lax.broadcasted_iota(jnp.int32, shape, dim)
    row = key % HALF
    owner = jnp.where(key < HALF, core, 1 - core)
    return (row // 16) * 32 + owner * 16 + row % 16


def place_of_head(head):
    row = 2 * LATENT + head // 4 * TOKENS
    return slice(row, row + TOKENS), slice(head % 4 * DIRECT, (head % 4 + 1) * DIRECT)


def absorb_kernel(
    info, query_ref, key_ref, latent_ref, length_ref, table_ref, pre_ref, value_ref, out, pre_out
):
    core = info[1]
    pre_out[:LATENT, :] = key_ref[...]
    pre_out[LATENT : 2 * LATENT, :] = value_ref[...]
    for head in range(HEADS):
        query = pre_ref[:, head // 2 * 2 * HEAD : (head // 2 + 1) * 2 * HEAD]
        query = query[:, head % 2 * HEAD : (head % 2 + 1) * HEAD]
        rope = query[:, NOPE:]
        rows, columns = place_of_head(head)
        pre_out[rows, columns] = jnp.concatenate([query[:, :NOPE], rope, rope], axis=1)
    for pair in range(HEADS // 2):
        both = query_ref[:, pair * 2 * HEAD : (pair + 1) * 2 * HEAD]
        for part in range(2):
            head = pair * 2 + part
            query = both[:, part * HEAD : (part + 1) * HEAD]
            key_map = key_ref[:, head * NOPE : (head + 1) * NOPE]
            rows = slice(head * QUERIES, (head + 1) * QUERIES)
            out[rows, :LATENT] = dot_t(query[:, :NOPE], key_map).astype(jnp.bfloat16)
            rope = query[:, NOPE:]
            out[rows, LATENT:] = jnp.concatenate([rope, rope], axis=1)
    rows = slice(NEWEST, NEWEST + QUERIES)
    out[rows, : LATENT + ROPE] = latent_ref[...]
    out[rows, LATENT + ROPE :] = jnp.zeros((QUERIES, ROPE), jnp.bfloat16)
    table = table_ref[...]
    pages = table.shape[1]
    page = lax.broadcasted_iota(jnp.int32, table.shape, 1)
    slot = jnp.zeros(table.shape, jnp.int32)
    for place in range(pages):
        slot = slot + jnp.where(table[:, place : place + 1] == page, place, 0)
    limit = jnp.clip(length_ref[...] - slot * PAGE, 0, PAGE).astype(jnp.float32)
    shape = (pages, POOL)
    key = lax.broadcasted_iota(jnp.int32, shape, 1)
    of = (key % HALF) // (PAGE // 2)
    owner = (lax.broadcasted_iota(jnp.int32, shape, 0) == of).astype(jnp.bfloat16)
    spread = dot(limit.astype(jnp.bfloat16), owner)
    token = (token_of_key((ROWS, POOL), 1, core) % PAGE).astype(jnp.float32)
    pool = jnp.where(token < spread, 0.0, hidden)
    mine = lax.broadcasted_iota(jnp.int32, (QUERIES, QUERIES), 0)
    theirs = lax.broadcasted_iota(jnp.int32, (QUERIES, QUERIES), 1)
    seen = (mine % ROWS == theirs % ROWS) & (theirs // ROWS <= mine // ROWS)
    bias = jnp.concatenate([pool] * STEPS, axis=0)
    bias = jnp.concatenate([bias, jnp.where(seen, 0.0, hidden)], axis=1).astype(jnp.bfloat16)
    for at in range(0, KEYS, WIDTH):
        part = bias[:, at : at + WIDTH]
        row = BIAS + at // WIDTH * QUERIES
        out[row : row + QUERIES, : part.shape[1]] = part


def absorb(info, queries, absorb_keys, step_latent, lengths, table, pre_queries, absorb_values):
    return pl.pallas_call(
        absorb_kernel,
        out_shape=(
            jax.ShapeDtypeStruct((BIAS + 4 * QUERIES, WIDTH), jnp.bfloat16),
            jax.ShapeDtypeStruct((2 * LATENT + 2 * TOKENS, HEADS * NOPE), jnp.bfloat16),
        ),
        in_specs=[smem] + [vmem] * 7,
        out_specs=(vmem, vmem),
        compiler_params=params(56),
        cost_estimate=pl.CostEstimate(
            flops=2 * 1024 * 128 * 512, bytes_accessed=5_000_000, transcendentals=0
        ),
        name="absorb",
    )(info, queries, absorb_keys, step_latent, lengths, table, pre_queries, absorb_values)


def softmax_rows(scores, bias, weights, start, count):
    bias_start = start % bias.shape[0]
    shifted = []
    at = 0
    for part in scores:
        size = part.shape[1]
        mask = bias[bias_start : bias_start + count, at : at + size]
        shifted.append(part[start : start + count, :] + mask)
        at += size
    largest = functools.reduce(
        jnp.maximum, [jnp.max(part, axis=1, keepdims=True) for part in shifted]
    )
    total = 0.0
    at = 0
    for part in shifted:
        expo = jnp.exp2(part * to_exp2 - largest * to_exp2)
        weights[start : start + count, at : at + part.shape[1]] = expo.astype(jnp.bfloat16)
        total = total + jnp.sum(expo, axis=1, keepdims=True)
        at += part.shape[1]
    return 1.0 / total


def prefill_kernel(info, own, other, ready, out_ref, latent, bias, *held):
    ctx, core = info[0], info[1]
    keys, values, scores, weights = held[:2], held[2:6], held[6:8], held[8:]
    unpack(own, latent, keys, 0)
    unpack(other, latent, keys, HALF)
    token = token_of_key((TOKENS, POOL), 1, core)
    query = ctx * TOKENS + lax.broadcasted_iota(jnp.int32, (TOKENS, POOL), 0)
    bias[...] = jnp.where(token <= query, 0.0, hidden)
    inverse = {}

    def make(head, at):
        columns = slice(head * NOPE, (head + 1) * NOPE)
        maps = [ready[:LATENT, columns], ready[LATENT : 2 * LATENT, columns]]
        maps = jnp.concatenate(maps, axis=1)
        made = dot(latent[at : at + CUT, :], maps).astype(jnp.bfloat16)
        keys[head % 2][at : at + CUT, :NOPE] = made[:, :NOPE]
        values[head % 4][at : at + CUT, :] = made[:, NOPE:]

    def score(head, at):
        query = ready[place_of_head(head)]
        scores[head % 2][:, at : at + CUT] = dot_t(query, keys[head % 2][at : at + CUT, :])

    def soften(head, start):
        part = softmax_rows([scores[head % 2]], bias, weights[head % 2], start, SOFT)
        inverse.setdefault(head, []).append(part)

    def mix(head):
        mixed = dot(weights[head % 2][...], values[head % 4][...])
        scaled = mixed * jnp.concatenate(inverse[head], axis=0)
        out_ref[:, head * VALUE_DIM : (head + 1) * VALUE_DIM] = scaled.astype(jnp.bfloat16)

    turns = TOKENS // SOFT
    cuts = POOL // CUT
    for stage in range(HEADS + 3):
        if 0 <= stage - 3 < HEADS:
            mix(stage - 3)
        for turn in range(turns):
            for cut in range(turn * cuts // turns, (turn + 1) * cuts // turns):
                if 0 <= stage - 1 < HEADS:
                    score(stage - 1, cut * CUT)
                if stage < HEADS:
                    make(stage, cut * CUT)
            if 0 <= stage - 2 < HEADS:
                soften(stage - 2, turn * SOFT)


def prefill(info, own, other, ready):
    return pl.pallas_call(
        prefill_kernel,
        out_shape=jax.ShapeDtypeStruct((TOKENS, HEADS * VALUE_DIM), jnp.bfloat16),
        in_specs=[smem] + [vmem] * 3,
        out_specs=vmem,
        scratch_shapes=[
            pltpu.VMEM((POOL, LATENT), jnp.bfloat16),
            pltpu.VMEM((TOKENS, POOL), jnp.float32),
            *[pltpu.VMEM((POOL, DIRECT), jnp.bfloat16)] * 2,
            *[pltpu.VMEM((POOL, VALUE_DIM), jnp.bfloat16)] * 4,
            *[pltpu.VMEM((TOKENS, POOL), jnp.float32)] * 2,
            *[pltpu.VMEM((TOKENS, POOL), jnp.bfloat16)] * 2,
        ],
        compiler_params=params(PREFILL_MIB),
        cost_estimate=pl.CostEstimate(
            flops=2 * 2048 * 2048 * 1024, bytes_accessed=10_000_000, transcendentals=2048 * 2048
        ),
        name="prefill",
    )(info, own, other, ready)


def early_kernel(own, ready_hbm, weight_hbm, scores, ready, weight, keys, sems):
    loads = [
        pltpu.make_async_copy(ready_hbm, ready, sems.at[0]),
        pltpu.make_async_copy(weight_hbm.at[:EARLY, :], weight, sems.at[1]),
    ]
    for load in loads:
        load.start()
    unpack(own, keys, [keys], 0)
    loads[0].wait()
    rows = 2 * QUERIES
    for item in range(HEADS // 2):
        for at in range(0, HALF, DECODE_CUT):
            queries = ready[item * rows : (item + 1) * rows, :]
            scores[item, :, at : at + DECODE_CUT] = dot_t(queries, keys[at : at + DECODE_CUT, :])
    loads[1].wait()


def early(own, ready, out_weight):
    return pl.pallas_call(
        early_kernel,
        out_shape=(
            pltpu.VMEM((HEADS // 2, 2 * QUERIES, HALF), jnp.float32),
            pltpu.VMEM(ready.shape, ready.dtype),
            pltpu.VMEM((EARLY, MODEL), jnp.bfloat16),
        ),
        in_specs=[vmem, hbm, hbm],
        out_specs=(vmem,) * 3,
        scratch_shapes=[
            pltpu.VMEM((HALF, WIDTH), jnp.bfloat16),
            pltpu.SemaphoreType.DMA((2,)),
        ],
        compiler_params=params(EARLY_MIB),
        cost_estimate=pl.CostEstimate(
            flops=2 * 1024 * 1024 * 640, bytes_accessed=12_000_000, transcendentals=0
        ),
        name="early",
    )(own, ready, out_weight)


def decode_kernel(
    info, own, other, early, ready, first_weight, value_ref, weight_hbm,
    keep_ref, send_ref, weight, sem, keys, bias, s0, s1, w0, w1, heads_out,
):
    core = info[1]
    load = pltpu.make_async_copy(weight_hbm.at[EARLY:, :], weight, sem)
    load.start()
    unpack(own, keys, [], 0)
    unpack(other, keys, [keys], HALF)
    keys[POOL:, :] = ready[NEWEST:BIAS, :]
    for at in range(0, KEYS, WIDTH):
        row = BIAS + at // WIDTH * QUERIES
        size = min(WIDTH, KEYS - at)
        bias[:, at : at + size] = ready[row : row + QUERIES, :size].astype(jnp.float32)
    scores, weights = (s0, s1), (w0, w1)
    inverse = {}
    items = HEADS // 2
    rows = 2 * QUERIES

    def score(item, at, size):
        queries = ready[item * rows : (item + 1) * rows, :]
        scores[item % 2][:, at - HALF : at - HALF + size] = dot_t(queries, keys[at : at + size, :])

    def soften(item, start):
        part = softmax_rows(
            [early.at[item], scores[item % 2]], bias, weights[item % 2], start, SOFT
        )
        inverse.setdefault(item, []).append(part)

    def mix(item):
        scale = jnp.concatenate(inverse[item], axis=0)
        mixed = [
            (dot(weights[item % 2][...], keys[:, at : at + 256]) * scale).astype(jnp.bfloat16)
            for at in range(0, LATENT, 256)
        ]
        mixed = jnp.concatenate(mixed, axis=1)
        for part in range(2):
            head = item * 2 + part
            columns = slice(head * VALUE_DIM, (head + 1) * VALUE_DIM)
            heads_out[:, columns] = dot(
                mixed[part * QUERIES : (part + 1) * QUERIES], value_ref[:, columns]
            ).astype(jnp.bfloat16)

    turns = rows // SOFT
    parts = [(at, min(DECODE_CUT, KEYS - at)) for at in range(HALF, KEYS, DECODE_CUT)]
    for stage in range(items + 2):
        if 0 <= stage - 2 < items:
            mix(stage - 2)
        for turn in range(turns):
            if stage < items:
                for at, size in parts[turn * len(parts) // turns : (turn + 1) * len(parts) // turns]:
                    score(stage, at, size)
            if 0 <= stage - 1 < items:
                soften(stage - 1, turn * SOFT)
    load.wait()

    for place in range(8):
        columns = slice(place * 2 * SHARE, (place + 1) * 2 * SHARE)
        turned = dot(heads_out[:, :EARLY], first_weight[:, columns])
        turned = (turned + dot(heads_out[:, EARLY:], weight[:, columns])).T
        first, second = turned[:SHARE], turned[SHARE:]
        keep_ref[place] = jnp.where(core == 0, first, second).astype(jnp.bfloat16)
        send_ref[place] = jnp.where(core == 0, second, first).astype(jnp.bfloat16)


def decode(info, own, other, scores, ready, first_weight, absorb_values, out_weight):
    share = jax.ShapeDtypeStruct((8, SHARE, QUERIES), jnp.bfloat16)
    return pl.pallas_call(
        decode_kernel,
        out_shape=(share, share),
        in_specs=[smem] + [vmem] * 6 + [hbm],
        out_specs=(vmem, vmem),
        scratch_shapes=[
            pltpu.VMEM((HEADS * VALUE_DIM - EARLY, MODEL), jnp.bfloat16),
            pltpu.SemaphoreType.DMA(()),
            pltpu.VMEM((KEYS, WIDTH), jnp.bfloat16),
            pltpu.VMEM((QUERIES, KEYS), jnp.float32),
            pltpu.VMEM((2 * QUERIES, KEYS - HALF), jnp.float32),
            pltpu.VMEM((2 * QUERIES, KEYS - HALF), jnp.float32),
            pltpu.VMEM((2 * QUERIES, KEYS), jnp.bfloat16),
            pltpu.VMEM((2 * QUERIES, KEYS), jnp.bfloat16),
            pltpu.VMEM((QUERIES, HEADS * VALUE_DIM), jnp.bfloat16),
        ],
        compiler_params=params(DECODE_MIB),
        cost_estimate=pl.CostEstimate(
            flops=2 * 1024 * 2176 * 1280 + 2 * 128 * 1024 * 7168,
            bytes_accessed=22_000_000,
            transcendentals=1024 * 2176,
        ),
        name="decode",
    )(info, own, other, scores, ready, first_weight, absorb_values, out_weight)


def gather_sum_kernel(parts, out_ref):
    total = parts[0].astype(jnp.float32)
    for place in range(1, parts.shape[0]):
        total = total + parts[place].astype(jnp.float32)
    out_ref[...] = total.T.astype(jnp.bfloat16)


def gather_sum(parts):
    return pl.pallas_call(
        gather_sum_kernel,
        out_shape=jax.ShapeDtypeStruct((QUERIES, SHARE), jnp.bfloat16),
        in_specs=[vmem],
        out_specs=vmem,
        compiler_params=params(16),
        name="gather_sum",
    )(parts)


def on_device(
    pre_queries,
    pre_latent,
    absorb_keys,
    absorb_values,
    step_queries,
    step_latent,
    context_lengths,
    page_table,
    out_weight,
):
    tp = lax.axis_index("tp")
    info = jnp.stack([lax.axis_index("ctx"), tp % 2]).astype(jnp.int32)
    own = lax.all_to_all(pack(pre_latent), BOTH, 0, 0, axis_index_groups=same_core_groups())
    ready, pre_ready = absorb(
        info,
        step_queries.reshape(QUERIES, HEADS * HEAD),
        absorb_keys,
        step_latent.reshape(QUERIES, LATENT + ROPE),
        context_lengths.reshape(ROWS, 1),
        page_table,
        pre_queries,
        absorb_values,
    )
    own, ready, pre_ready = lax.optimization_barrier((own, ready, pre_ready))
    other = lax.ppermute(own, BOTH, other_core())
    scores, ready, first_weight = early(own, ready, out_weight)
    keep, send = decode(
        info, own, other, scores, ready, first_weight, absorb_values, out_weight
    )
    arrived = lax.ppermute(send, BOTH, other_core())
    chip = (keep.astype(jnp.float32) + arrived.astype(jnp.float32)).astype(jnp.bfloat16)
    chip, own, other = lax.optimization_barrier((chip, own, other))
    parts = lax.all_to_all(chip, BOTH, 0, 0, axis_index_groups=chip_groups())
    prefill_heads = prefill(info, own, other, pre_ready)
    decode_out = gather_sum(parts).reshape(STEPS, ROWS, SHARE)
    return (prefill_heads, decode_out)


def solution(mesh):
    return jax.shard_map(
        on_device,
        mesh=mesh,
        in_specs=(
            P("ctx", "tp"),
            P(("ctx", "tp"), None),
            P(None, "tp"),
            P(None, "tp"),
            P(None, "ctx", "tp"),
            P(None, "ctx", None),
            P("ctx"),
            P("ctx", None),
            P("tp", None),
        ),
        out_specs=(P("ctx", "tp"), P(None, "ctx", "tp")),
        check_vma=False,
    )
```

```python
import functools
import itertools
import math

import jax
import jax.numpy as jnp
from jax import lax
from jax.experimental import pallas as pl
from jax.experimental.pallas import tpu as pltpu
from jax.sharding import PartitionSpec as P

LATENT = 512
ROPE = 64
NOPE = 128
VALUE_DIM = 128
PAGE = 64
STEPS = 4
WIDTH = LATENT + 2 * ROPE
DIRECT = NOPE + 2 * ROPE
PIECE = 72
HALF = 1024
HEAD = NOPE + ROPE
HEADS = 8
TOKENS = 256
ROWS = 32
QUERIES = STEPS * ROWS
POOL = 2048
KEYS = POOL + QUERIES
MODEL = 7168
SHARE = 448
BOTH = ("ctx", "tp")
NEWEST = HEADS * QUERIES
BIAS = NEWEST + QUERIES

hidden = -1e30
CUT = 1024
SOFT = 16
DECODE_CUT = 256
PREFILL_MIB = 48
DECODE_MIB = 24
KEEP_MIB = 24
EARLY_MIB = 43
EARLY = 256
to_exp2 = math.log2(math.e) / math.sqrt(HEAD)
vmem = pl.BlockSpec(memory_space=pltpu.VMEM)
smem = pl.BlockSpec(memory_space=pltpu.SMEM)
hbm = pl.BlockSpec(memory_space=pltpu.HBM)


def params(mib):
    return pltpu.CompilerParams(vmem_limit_bytes=mib * 1024 * 1024)


def flat(x, y, z, core):
    return (x * 2 + y // 2) * 16 + z * 4 + (y % 2) * 2 + core


def chips():
    return itertools.product(range(4), range(4), range(4), range(2))


def chip_groups():
    return [
        [flat(x, yh * 2 + yl, z, core) for z, yl in itertools.product(range(4), range(2))]
        for x, yh, core in itertools.product(range(4), range(2), range(2))
    ]


def other_core():
    return [(flat(x, y, z, c), flat(x, y, z, 1 - c)) for x, y, z, c in chips()]


def same_core_groups():
    return [
        [
            flat(x, yh * 2 + yl, z, core)
            for x, yh, z, yl in itertools.product(range(4), range(2), range(4), range(2))
        ]
        for core in range(2)
    ]


def dot(a, b):
    return jnp.dot(a, b, preferred_element_type=jnp.float32)


def dot_t(a, b):
    return lax.dot_general(a, b, (((1,), (1,)), ((), ())), preferred_element_type=jnp.float32)


def pack_kernel(latent_ref, out_ref):
    late = (lax.axis_index("tp") // 2) % 2
    latent = latent_ref[...].astype(jnp.float32)
    rope = latent[:, LATENT:]
    parts = [latent[:, at : at + 128] for at in range(0, LATENT, 128)]
    rope = jnp.concatenate([rope[:8], rope[8:]], axis=1)
    piece = jnp.where(
        late == 0, jnp.concatenate([*parts, rope], axis=0), jnp.concatenate([rope, *parts], axis=0)
    )
    two = jnp.concatenate([piece, piece], axis=0).astype(jnp.bfloat16)
    for place in range(32):
        out_ref[place] = two


def pack(latent):
    return pl.pallas_call(
        pack_kernel,
        out_shape=jax.ShapeDtypeStruct((32, 2 * PIECE, 128), jnp.bfloat16),
        in_specs=[vmem],
        out_specs=vmem,
        compiler_params=params(16),
        name="pack",
    )(latent)


def unpack(source, latent, ropes, at):
    for pair in range(0, 32, 4):
        rows = slice(at + pair * 32, at + pair * 32 + 128)
        pairs = slice(pair, pair + 4)
        for tile in range(4):
            first = source[pairs, tile * 16 : (tile + 1) * 16, :]
            second = source[pairs, 80 + tile * 16 : 96 + tile * 16, :]
            latent[rows, tile * 128 : (tile + 1) * 128] = jnp.stack([first, second], axis=1).reshape(
                128, 128
            )
        rope = source[pairs, 64:80, :].astype(jnp.float32).reshape(8, 8, 128)
        left = lax.broadcasted_iota(jnp.int32, rope.shape, 2) < ROPE
        both = jnp.concatenate([jnp.where(left, rope, 0.0), jnp.where(left, 0.0, rope)], axis=1)
        both = both.reshape(128, 128).astype(jnp.bfloat16)
        for ref in ropes:
            ref[rows, ref.shape[1] - 2 * ROPE :] = both


def token_of_key(shape, dim, core):
    key = lax.broadcasted_iota(jnp.int32, shape, dim)
    row = key % HALF
    owner = jnp.where(key < HALF, core, 1 - core)
    return (row // 16) * 32 + owner * 16 + row % 16


def place_of_head(head):
    row = 2 * LATENT + head // 4 * TOKENS
    return slice(row, row + TOKENS), slice(head % 4 * DIRECT, (head % 4 + 1) * DIRECT)


def absorb_kernel(
    info, query_ref, key_ref, latent_ref, length_ref, table_ref, pre_ref, value_ref, out, pre_out
):
    core = info[1]
    pre_out[:LATENT, :] = key_ref[...]
    pre_out[LATENT : 2 * LATENT, :] = value_ref[...]
    for head in range(HEADS):
        query = pre_ref[:, head // 2 * 2 * HEAD : (head // 2 + 1) * 2 * HEAD]
        query = query[:, head % 2 * HEAD : (head % 2 + 1) * HEAD]
        rope = query[:, NOPE:]
        rows, columns = place_of_head(head)
        pre_out[rows, columns] = jnp.concatenate([query[:, :NOPE], rope, rope], axis=1)
    for pair in range(HEADS // 2):
        both = query_ref[:, pair * 2 * HEAD : (pair + 1) * 2 * HEAD]
        for part in range(2):
            head = pair * 2 + part
            query = both[:, part * HEAD : (part + 1) * HEAD]
            key_map = key_ref[:, head * NOPE : (head + 1) * NOPE]
            rows = slice(head * QUERIES, (head + 1) * QUERIES)
            out[rows, :LATENT] = dot_t(query[:, :NOPE], key_map).astype(jnp.bfloat16)
            rope = query[:, NOPE:]
            out[rows, LATENT:] = jnp.concatenate([rope, rope], axis=1)
    rows = slice(NEWEST, NEWEST + QUERIES)
    out[rows, : LATENT + ROPE] = latent_ref[...]
    out[rows, LATENT + ROPE :] = jnp.zeros((QUERIES, ROPE), jnp.bfloat16)
    table = table_ref[...]
    pages = table.shape[1]
    page = lax.broadcasted_iota(jnp.int32, table.shape, 1)
    slot = jnp.zeros(table.shape, jnp.int32)
    for place in range(pages):
        slot = slot + jnp.where(table[:, place : place + 1] == page, place, 0)
    limit = jnp.clip(length_ref[...] - slot * PAGE, 0, PAGE).astype(jnp.float32)
    shape = (pages, POOL)
    key = lax.broadcasted_iota(jnp.int32, shape, 1)
    of = (key % HALF) // (PAGE // 2)
    owner = (lax.broadcasted_iota(jnp.int32, shape, 0) == of).astype(jnp.bfloat16)
    spread = dot(limit.astype(jnp.bfloat16), owner)
    token = (token_of_key((ROWS, POOL), 1, core) % PAGE).astype(jnp.float32)
    pool = jnp.where(token < spread, 0.0, hidden)
    mine = lax.broadcasted_iota(jnp.int32, (QUERIES, QUERIES), 0)
    theirs = lax.broadcasted_iota(jnp.int32, (QUERIES, QUERIES), 1)
    seen = (mine % ROWS == theirs % ROWS) & (theirs // ROWS <= mine // ROWS)
    bias = jnp.concatenate([pool] * STEPS, axis=0)
    bias = jnp.concatenate([bias, jnp.where(seen, 0.0, hidden)], axis=1).astype(jnp.bfloat16)
    for at in range(0, KEYS, WIDTH):
        part = bias[:, at : at + WIDTH]
        row = BIAS + at // WIDTH * QUERIES
        out[row : row + QUERIES, : part.shape[1]] = part


def absorb(info, queries, absorb_keys, step_latent, lengths, table, pre_queries, absorb_values):
    return pl.pallas_call(
        absorb_kernel,
        out_shape=(
            jax.ShapeDtypeStruct((BIAS + 4 * QUERIES, WIDTH), jnp.bfloat16),
            jax.ShapeDtypeStruct((2 * LATENT + 2 * TOKENS, HEADS * NOPE), jnp.bfloat16),
        ),
        in_specs=[smem] + [vmem] * 7,
        out_specs=(vmem, vmem),
        compiler_params=params(56),
        cost_estimate=pl.CostEstimate(
            flops=2 * 1024 * 128 * 512, bytes_accessed=5_000_000, transcendentals=0
        ),
        name="absorb",
    )(info, queries, absorb_keys, step_latent, lengths, table, pre_queries, absorb_values)


def softmax_rows(scores, bias, weights, start, count):
    bias_start = start % bias.shape[0]
    shifted = []
    at = 0
    for part in scores:
        size = part.shape[1]
        mask = bias[bias_start : bias_start + count, at : at + size]
        shifted.append(part[start : start + count, :] + mask)
        at += size
    largest = functools.reduce(
        jnp.maximum, [jnp.max(part, axis=1, keepdims=True) for part in shifted]
    )
    total = 0.0
    at = 0
    for part in shifted:
        expo = jnp.exp2(part * to_exp2 - largest * to_exp2)
        weights[start : start + count, at : at + part.shape[1]] = expo.astype(jnp.bfloat16)
        total = total + jnp.sum(expo, axis=1, keepdims=True)
        at += part.shape[1]
    return 1.0 / total


def prefill_kernel(info, own, other, ready, out_ref, latent, bias, *held):
    ctx, core = info[0], info[1]
    keys, values, scores, weights = held[:2], held[2:6], held[6:8], held[8:]
    unpack(own, latent, keys, 0)
    unpack(other, latent, keys, HALF)
    token = token_of_key((TOKENS, POOL), 1, core)
    query = ctx * TOKENS + lax.broadcasted_iota(jnp.int32, (TOKENS, POOL), 0)
    bias[...] = jnp.where(token <= query, 0.0, hidden)
    inverse = {}

    def make(head, at):
        columns = slice(head * NOPE, (head + 1) * NOPE)
        maps = [ready[:LATENT, columns], ready[LATENT : 2 * LATENT, columns]]
        maps = jnp.concatenate(maps, axis=1)
        made = dot(latent[at : at + CUT, :], maps).astype(jnp.bfloat16)
        keys[head % 2][at : at + CUT, :NOPE] = made[:, :NOPE]
        values[head % 4][at : at + CUT, :] = made[:, NOPE:]

    def score(head, at):
        query = ready[place_of_head(head)]
        scores[head % 2][:, at : at + CUT] = dot_t(query, keys[head % 2][at : at + CUT, :])

    def soften(head, start):
        part = softmax_rows([scores[head % 2]], bias, weights[head % 2], start, SOFT)
        inverse.setdefault(head, []).append(part)

    def mix(head):
        mixed = dot(weights[head % 2][...], values[head % 4][...])
        scaled = mixed * jnp.concatenate(inverse[head], axis=0)
        out_ref[:, head * VALUE_DIM : (head + 1) * VALUE_DIM] = scaled.astype(jnp.bfloat16)

    turns = TOKENS // SOFT
    cuts = POOL // CUT
    for stage in range(HEADS + 3):
        if 0 <= stage - 3 < HEADS:
            mix(stage - 3)
        for turn in range(turns):
            for cut in range(turn * cuts // turns, (turn + 1) * cuts // turns):
                if 0 <= stage - 1 < HEADS:
                    score(stage - 1, cut * CUT)
                if stage < HEADS:
                    make(stage, cut * CUT)
            if 0 <= stage - 2 < HEADS:
                soften(stage - 2, turn * SOFT)


def prefill(info, own, other, ready):
    return pl.pallas_call(
        prefill_kernel,
        out_shape=jax.ShapeDtypeStruct((TOKENS, HEADS * VALUE_DIM), jnp.bfloat16),
        in_specs=[smem] + [vmem] * 3,
        out_specs=vmem,
        scratch_shapes=[
            pltpu.VMEM((POOL, LATENT), jnp.bfloat16),
            pltpu.VMEM((TOKENS, POOL), jnp.float32),
            *[pltpu.VMEM((POOL, DIRECT), jnp.bfloat16)] * 2,
            *[pltpu.VMEM((POOL, VALUE_DIM), jnp.bfloat16)] * 4,
            *[pltpu.VMEM((TOKENS, POOL), jnp.float32)] * 2,
            *[pltpu.VMEM((TOKENS, POOL), jnp.bfloat16)] * 2,
        ],
        compiler_params=params(PREFILL_MIB),
        cost_estimate=pl.CostEstimate(
            flops=2 * 2048 * 2048 * 1024, bytes_accessed=10_000_000, transcendentals=2048 * 2048
        ),
        name="prefill",
    )(info, own, other, ready)


def early_kernel(own, ready_hbm, weight_hbm, scores, ready, weight, keys, sems):
    loads = [
        pltpu.make_async_copy(ready_hbm.at[:NEWEST, :], ready.at[:NEWEST, :], sems.at[0]),
        pltpu.make_async_copy(ready_hbm.at[NEWEST:, :], ready.at[NEWEST:, :], sems.at[1]),
        pltpu.make_async_copy(weight_hbm.at[:EARLY, :], weight, sems.at[2]),
    ]
    for load in loads:
        load.start()
    unpack(own, keys, [keys], 0)
    loads[0].wait()
    rows = 2 * QUERIES
    for item in range(HEADS // 2):
        for at in range(0, HALF, DECODE_CUT):
            queries = ready[item * rows : (item + 1) * rows, :]
            scores[item, :, at : at + DECODE_CUT] = dot_t(queries, keys[at : at + DECODE_CUT, :])
    loads[1].wait()
    loads[2].wait()


def early(own, ready, out_weight):
    return pl.pallas_call(
        early_kernel,
        out_shape=(
            pltpu.VMEM((HEADS // 2, 2 * QUERIES, HALF), jnp.float32),
            pltpu.VMEM(ready.shape, ready.dtype),
            pltpu.VMEM((EARLY, MODEL), jnp.bfloat16),
        ),
        in_specs=[vmem, hbm, hbm],
        out_specs=(vmem,) * 3,
        scratch_shapes=[
            pltpu.VMEM((HALF, WIDTH), jnp.bfloat16),
            pltpu.SemaphoreType.DMA((3,)),
        ],
        compiler_params=params(EARLY_MIB),
        cost_estimate=pl.CostEstimate(
            flops=2 * 1024 * 1024 * 640, bytes_accessed=12_000_000, transcendentals=0
        ),
        name="early",
    )(own, ready, out_weight)


def decode_kernel(
    info, own, other, early, ready, first_weight, value_ref, weight_hbm,
    send_ref, heads_out, weight, sems, partial, keys, bias, s0, s1, w0, w1,
):
    core = info[1]
    loads = [
        pltpu.make_async_copy(
            weight_hbm.at[at : at + size, :], weight.at[at - EARLY : at - EARLY + size, :], sem
        )
        for at, size, sem in ((EARLY, 256, sems.at[0]), (EARLY + 256, 512, sems.at[1]))
    ]
    for load in loads:
        load.start()
    unpack(own, keys, [], 0)
    unpack(other, keys, [keys], HALF)
    keys[POOL:, :] = ready[NEWEST:BIAS, :]
    for at in range(0, KEYS, WIDTH):
        row = BIAS + at // WIDTH * QUERIES
        size = min(WIDTH, KEYS - at)
        bias[:, at : at + size] = ready[row : row + QUERIES, :size].astype(jnp.float32)
    scores, weights = (s0, s1), (w0, w1)
    inverse = {}
    items = HEADS // 2
    rows = 2 * QUERIES

    def score(item, at, size):
        queries = ready[item * rows : (item + 1) * rows, :]
        scores[item % 2][:, at - HALF : at - HALF + size] = dot_t(queries, keys[at : at + size, :])

    def soften(item, start):
        part = softmax_rows(
            [early.at[item], scores[item % 2]], bias, weights[item % 2], start, SOFT
        )
        inverse.setdefault(item, []).append(part)

    def mix(item):
        scale = jnp.concatenate(inverse[item], axis=0)
        mixed = [
            (dot(weights[item % 2][...], keys[:, at : at + 256]) * scale).astype(jnp.bfloat16)
            for at in range(0, LATENT, 256)
        ]
        mixed = jnp.concatenate(mixed, axis=1)
        for part in range(2):
            head = item * 2 + part
            columns = slice(head * VALUE_DIM, (head + 1) * VALUE_DIM)
            heads_out[:, columns] = dot(
                mixed[part * QUERIES : (part + 1) * QUERIES], value_ref[:, columns]
            ).astype(jnp.bfloat16)

    turns = rows // SOFT
    parts = [(at, min(DECODE_CUT, KEYS - at)) for at in range(HALF, KEYS, DECODE_CUT)]
    for stage in range(items + 2):
        if 0 <= stage - 2 < items:
            mix(stage - 2)
        if stage == items:
            loads[0].wait()
            for place in range(8):
                columns = columns_for(place, 1 - core)
                partial[place] = dot(heads_out[:, :EARLY], first_weight[:, columns]) + dot(
                    heads_out[:, EARLY : EARLY + 256], weight[:256, columns]
                )
        for turn in range(turns):
            if stage < items:
                for at, size in parts[turn * len(parts) // turns : (turn + 1) * len(parts) // turns]:
                    score(stage, at, size)
            if 0 <= stage - 1 < items:
                soften(stage - 1, turn * SOFT)
    loads[1].wait()
    for place in range(8):
        rest = dot(heads_out[:, EARLY + 256 :], weight[256:, columns_for(place, 1 - core)])
        send_ref[place] = turned(partial[place] + rest, 1 - core)


def columns_for(place, core):
    start = place * 2 * SHARE + core * (SHARE - 64)
    return pl.ds(pl.multiple_of(start, 128), SHARE + 64)


def turned(product, core):
    columns = product.T
    return jnp.where(core == 0, columns[:SHARE], columns[64:]).astype(jnp.bfloat16)


def keep_kernel(info, heads_out, first_weight, weight, keep_ref):
    core = info[1]
    for place in range(8):
        columns = columns_for(place, core)
        product = dot(heads_out[:, :EARLY], first_weight[:, columns])
        product = product + dot(heads_out[:, EARLY:], weight[:, columns])
        keep_ref[place] = turned(product, core)


def own_share(info, heads_out, first_weight, weight):
    return pl.pallas_call(
        keep_kernel,
        out_shape=jax.ShapeDtypeStruct((8, SHARE, QUERIES), jnp.bfloat16),
        in_specs=[smem] + [vmem] * 3,
        out_specs=vmem,
        compiler_params=params(KEEP_MIB),
        cost_estimate=pl.CostEstimate(
            flops=2 * 128 * 1024 * 4096, bytes_accessed=8_000_000, transcendentals=0
        ),
        name="own_share",
    )(info, heads_out, first_weight, weight)


def decode(info, own, other, scores, ready, first_weight, absorb_values, out_weight):
    width = HEADS * VALUE_DIM
    return pl.pallas_call(
        decode_kernel,
        out_shape=(
            jax.ShapeDtypeStruct((8, SHARE, QUERIES), jnp.bfloat16),
            pltpu.VMEM((QUERIES, width), jnp.bfloat16),
            pltpu.VMEM((width - EARLY, MODEL), jnp.bfloat16),
        ),
        in_specs=[smem] + [vmem] * 6 + [hbm],
        out_specs=(vmem,) * 3,
        scratch_shapes=[
            pltpu.SemaphoreType.DMA((2,)),
            pltpu.VMEM((8, QUERIES, SHARE + 64), jnp.float32),
            pltpu.VMEM((KEYS, WIDTH), jnp.bfloat16),
            pltpu.VMEM((QUERIES, KEYS), jnp.float32),
            pltpu.VMEM((2 * QUERIES, KEYS - HALF), jnp.float32),
            pltpu.VMEM((2 * QUERIES, KEYS - HALF), jnp.float32),
            pltpu.VMEM((2 * QUERIES, KEYS), jnp.bfloat16),
            pltpu.VMEM((2 * QUERIES, KEYS), jnp.bfloat16),
        ],
        compiler_params=params(DECODE_MIB),
        cost_estimate=pl.CostEstimate(
            flops=2 * 1024 * 2176 * 1280 + 2 * 128 * 1024 * 7168,
            bytes_accessed=22_000_000,
            transcendentals=1024 * 2176,
        ),
        name="decode",
    )(info, own, other, scores, ready, first_weight, absorb_values, out_weight)


def gather_sum_kernel(parts, out_ref):
    total = parts[0].astype(jnp.float32)
    for place in range(1, parts.shape[0]):
        total = total + parts[place].astype(jnp.float32)
    out_ref[...] = total.T.astype(jnp.bfloat16)


def gather_sum(parts):
    return pl.pallas_call(
        gather_sum_kernel,
        out_shape=jax.ShapeDtypeStruct((QUERIES, SHARE), jnp.bfloat16),
        in_specs=[vmem],
        out_specs=vmem,
        compiler_params=params(16),
        name="gather_sum",
    )(parts)


def on_device(
    pre_queries,
    pre_latent,
    absorb_keys,
    absorb_values,
    step_queries,
    step_latent,
    context_lengths,
    page_table,
    out_weight,
):
    tp = lax.axis_index("tp")
    info = jnp.stack([lax.axis_index("ctx"), tp % 2]).astype(jnp.int32)
    pieces = pack(pre_latent).reshape(64, PIECE, 128)
    own = lax.all_to_all(pieces, BOTH, 0, 0, axis_index_groups=same_core_groups())
    own = own.reshape(32, 2 * PIECE, 128)
    ready, pre_ready = absorb(
        info,
        step_queries.reshape(QUERIES, HEADS * HEAD),
        absorb_keys,
        step_latent.reshape(QUERIES, LATENT + ROPE),
        context_lengths.reshape(ROWS, 1),
        page_table,
        pre_queries,
        absorb_values,
    )
    own, ready, pre_ready = lax.optimization_barrier((own, ready, pre_ready))
    other = lax.ppermute(own, BOTH, other_core())
    scores, ready, first_weight = early(own, ready, out_weight)
    send, heads_out, weight = decode(
        info, own, other, scores, ready, first_weight, absorb_values, out_weight
    )
    arrived = lax.ppermute(send, BOTH, other_core())
    keep = own_share(info, heads_out, first_weight, weight)
    chip = (keep.astype(jnp.float32) + arrived.astype(jnp.float32)).astype(jnp.bfloat16)
    chip, own, other = lax.optimization_barrier((chip, own, other))
    parts = lax.all_to_all(chip, BOTH, 0, 0, axis_index_groups=chip_groups())
    prefill_heads = prefill(info, own, other, pre_ready)
    decode_out = gather_sum(parts).reshape(STEPS, ROWS, SHARE)
    return (prefill_heads, decode_out)


def solution(mesh):
    return jax.shard_map(
        on_device,
        mesh=mesh,
        in_specs=(
            P("ctx", "tp"),
            P(("ctx", "tp"), None),
            P(None, "tp"),
            P(None, "tp"),
            P(None, "ctx", "tp"),
            P(None, "ctx", None),
            P("ctx"),
            P("ctx", None),
            P("tp", None),
        ),
        out_specs=(P("ctx", "tp"), P(None, "ctx", "tp")),
        check_vma=False,
    )
```

```python
import functools
import itertools
import math

import jax
import jax.numpy as jnp
from jax import lax
from jax.experimental import pallas as pl
from jax.experimental.pallas import tpu as pltpu
from jax.sharding import PartitionSpec as P

LATENT = 512
ROPE = 64
NOPE = 128
VALUE_DIM = 128
PAGE = 64
STEPS = 4
WIDTH = LATENT + 2 * ROPE
DIRECT = NOPE + 2 * ROPE
PIECE = 72
HALF = 1024
HEAD = NOPE + ROPE
HEADS = 8
TOKENS = 256
ROWS = 32
QUERIES = STEPS * ROWS
POOL = 2048
KEYS = POOL + QUERIES
MODEL = 7168
SHARE = 448
BOTH = ("ctx", "tp")
NEWEST = HEADS * QUERIES
BIAS = NEWEST + QUERIES

hidden = -1e30
CUT = 1024
SOFT = 16
DECODE_CUT = 256
PREFILL_MIB = 48
DECODE_MIB = 24
KEEP_MIB = 24
EARLY_MIB = 43
EARLY = 256
to_exp2 = math.log2(math.e) / math.sqrt(HEAD)
vmem = pl.BlockSpec(memory_space=pltpu.VMEM)
hbm = pl.BlockSpec(memory_space=pltpu.HBM)


def params(mib):
    return pltpu.CompilerParams(vmem_limit_bytes=mib * 1024 * 1024)


def flat(x, y, z, core):
    return (x * 2 + y // 2) * 16 + z * 4 + (y % 2) * 2 + core


def chips():
    return itertools.product(range(4), range(4), range(4), range(2))


def chip_groups():
    return [
        [flat(x, yh * 2 + yl, z, core) for z, yl in itertools.product(range(4), range(2))]
        for x, yh, core in itertools.product(range(4), range(2), range(2))
    ]


def other_core():
    return [(flat(x, y, z, c), flat(x, y, z, 1 - c)) for x, y, z, c in chips()]


def same_core_groups():
    return [
        [
            flat(x, yh * 2 + yl, z, core)
            for x, yh, z, yl in itertools.product(range(4), range(2), range(4), range(2))
        ]
        for core in range(2)
    ]


def own_core():
    return lax.axis_index("tp") % 2


def dot(a, b):
    return jnp.dot(a, b, preferred_element_type=jnp.float32)


def dot_t(a, b):
    return lax.dot_general(a, b, (((1,), (1,)), ((), ())), preferred_element_type=jnp.float32)


def pack_kernel(latent_ref, out_ref):
    late = (lax.axis_index("tp") // 2) % 2
    latent = latent_ref[...].astype(jnp.float32)
    rope = latent[:, LATENT:]
    parts = [latent[:, at : at + 128] for at in range(0, LATENT, 128)]
    rope = jnp.concatenate([rope[:8], rope[8:]], axis=1)
    piece = jnp.where(
        late == 0, jnp.concatenate([*parts, rope], axis=0), jnp.concatenate([rope, *parts], axis=0)
    )
    two = jnp.concatenate([piece, piece], axis=0).astype(jnp.bfloat16)
    for place in range(32):
        out_ref[place] = two


def pack(latent):
    return pl.pallas_call(
        pack_kernel,
        out_shape=jax.ShapeDtypeStruct((32, 2 * PIECE, 128), jnp.bfloat16),
        in_specs=[vmem],
        out_specs=vmem,
        compiler_params=params(16),
        name="pack",
    )(latent)


def unpack(source, latent, ropes, at):
    for pair in range(0, 32, 4):
        rows = slice(at + pair * 32, at + pair * 32 + 128)
        pairs = slice(pair, pair + 4)
        for tile in range(4):
            first = source[pairs, tile * 16 : (tile + 1) * 16, :]
            second = source[pairs, 80 + tile * 16 : 96 + tile * 16, :]
            latent[rows, tile * 128 : (tile + 1) * 128] = jnp.stack([first, second], axis=1).reshape(
                128, 128
            )
        rope = source[pairs, 64:80, :].astype(jnp.float32).reshape(8, 8, 128)
        left = lax.broadcasted_iota(jnp.int32, rope.shape, 2) < ROPE
        both = jnp.concatenate([jnp.where(left, rope, 0.0), jnp.where(left, 0.0, rope)], axis=1)
        both = both.reshape(128, 128).astype(jnp.bfloat16)
        for ref in ropes:
            ref[rows, ref.shape[1] - 2 * ROPE :] = both


def token_of_key(shape, dim, core):
    key = lax.broadcasted_iota(jnp.int32, shape, dim)
    row = key % HALF
    owner = jnp.where(key < HALF, core, 1 - core)
    return (row // 16) * 32 + owner * 16 + row % 16


def place_of_head(head):
    row = 2 * LATENT + head // 4 * TOKENS
    return slice(row, row + TOKENS), slice(head % 4 * DIRECT, (head % 4 + 1) * DIRECT)


def absorb_kernel(
    query_ref, key_ref, latent_ref, length_ref, table_ref, pre_ref, value_ref, out, pre_out
):
    core = own_core()
    pre_out[:LATENT, :] = key_ref[...]
    pre_out[LATENT : 2 * LATENT, :] = value_ref[...]
    for head in range(HEADS):
        query = pre_ref[:, head // 2 * 2 * HEAD : (head // 2 + 1) * 2 * HEAD]
        query = query[:, head % 2 * HEAD : (head % 2 + 1) * HEAD]
        rope = query[:, NOPE:]
        rows, columns = place_of_head(head)
        pre_out[rows, columns] = jnp.concatenate([query[:, :NOPE], rope, rope], axis=1)
    for pair in range(HEADS // 2):
        both = query_ref[:, pair * 2 * HEAD : (pair + 1) * 2 * HEAD]
        for part in range(2):
            head = pair * 2 + part
            query = both[:, part * HEAD : (part + 1) * HEAD]
            key_map = key_ref[:, head * NOPE : (head + 1) * NOPE]
            rows = slice(head * QUERIES, (head + 1) * QUERIES)
            out[rows, :LATENT] = dot_t(query[:, :NOPE], key_map).astype(jnp.bfloat16)
            rope = query[:, NOPE:]
            out[rows, LATENT:] = jnp.concatenate([rope, rope], axis=1)
    rows = slice(NEWEST, NEWEST + QUERIES)
    out[rows, : LATENT + ROPE] = latent_ref[...]
    out[rows, LATENT + ROPE :] = jnp.zeros((QUERIES, ROPE), jnp.bfloat16)
    table = table_ref[...]
    pages = table.shape[1]
    page = lax.broadcasted_iota(jnp.int32, table.shape, 1)
    slot = jnp.zeros(table.shape, jnp.int32)
    for place in range(pages):
        slot = slot + jnp.where(table[:, place : place + 1] == page, place, 0)
    limit = jnp.clip(length_ref[...] - slot * PAGE, 0, PAGE).astype(jnp.float32)
    shape = (pages, POOL)
    key = lax.broadcasted_iota(jnp.int32, shape, 1)
    of = (key % HALF) // (PAGE // 2)
    owner = (lax.broadcasted_iota(jnp.int32, shape, 0) == of).astype(jnp.bfloat16)
    spread = dot(limit.astype(jnp.bfloat16), owner)
    token = (token_of_key((ROWS, POOL), 1, core) % PAGE).astype(jnp.float32)
    pool = jnp.where(token < spread, 0.0, hidden)
    mine = lax.broadcasted_iota(jnp.int32, (QUERIES, QUERIES), 0)
    theirs = lax.broadcasted_iota(jnp.int32, (QUERIES, QUERIES), 1)
    seen = (mine % ROWS == theirs % ROWS) & (theirs // ROWS <= mine // ROWS)
    bias = jnp.concatenate([pool] * STEPS, axis=0)
    bias = jnp.concatenate([bias, jnp.where(seen, 0.0, hidden)], axis=1).astype(jnp.bfloat16)
    for at in range(0, KEYS, WIDTH):
        part = bias[:, at : at + WIDTH]
        row = BIAS + at // WIDTH * QUERIES
        out[row : row + QUERIES, : part.shape[1]] = part


def absorb(queries, absorb_keys, step_latent, lengths, table, pre_queries, absorb_values):
    return pl.pallas_call(
        absorb_kernel,
        out_shape=(
            jax.ShapeDtypeStruct((BIAS + 4 * QUERIES, WIDTH), jnp.bfloat16),
            jax.ShapeDtypeStruct((2 * LATENT + 2 * TOKENS, HEADS * NOPE), jnp.bfloat16),
        ),
        in_specs=[vmem] * 7,
        out_specs=(vmem, vmem),
        compiler_params=params(56),
        cost_estimate=pl.CostEstimate(
            flops=2 * 1024 * 128 * 512, bytes_accessed=5_000_000, transcendentals=0
        ),
        name="absorb",
    )(queries, absorb_keys, step_latent, lengths, table, pre_queries, absorb_values)


def softmax_rows(scores, bias, weights, start, count):
    bias_start = start % bias.shape[0]
    shifted = []
    at = 0
    for part in scores:
        size = part.shape[1]
        mask = bias[bias_start : bias_start + count, at : at + size]
        shifted.append(part[start : start + count, :] + mask)
        at += size
    largest = functools.reduce(
        jnp.maximum, [jnp.max(part, axis=1, keepdims=True) for part in shifted]
    )
    total = 0.0
    at = 0
    for part in shifted:
        expo = jnp.exp2(part * to_exp2 - largest * to_exp2)
        weights[start : start + count, at : at + part.shape[1]] = expo.astype(jnp.bfloat16)
        total = total + jnp.sum(expo, axis=1, keepdims=True)
        at += part.shape[1]
    return 1.0 / total


def prefill_kernel(own, other, ready, out_ref, latent, bias, *held):
    ctx, core = lax.axis_index("ctx"), own_core()
    keys, values, scores, weights = held[:2], held[2:6], held[6:8], held[8:]
    unpack(own, latent, keys, 0)
    unpack(other, latent, keys, HALF)
    token = token_of_key((TOKENS, POOL), 1, core)
    query = ctx * TOKENS + lax.broadcasted_iota(jnp.int32, (TOKENS, POOL), 0)
    bias[...] = jnp.where(token <= query, 0.0, hidden)
    inverse = {}

    def make(head, at):
        columns = slice(head * NOPE, (head + 1) * NOPE)
        maps = [ready[:LATENT, columns], ready[LATENT : 2 * LATENT, columns]]
        maps = jnp.concatenate(maps, axis=1)
        made = dot(latent[at : at + CUT, :], maps).astype(jnp.bfloat16)
        keys[head % 2][at : at + CUT, :NOPE] = made[:, :NOPE]
        values[head % 4][at : at + CUT, :] = made[:, NOPE:]

    def score(head, at):
        query = ready[place_of_head(head)]
        scores[head % 2][:, at : at + CUT] = dot_t(query, keys[head % 2][at : at + CUT, :])

    def soften(head, start):
        part = softmax_rows([scores[head % 2]], bias, weights[head % 2], start, SOFT)
        inverse.setdefault(head, []).append(part)

    def mix(head):
        mixed = dot(weights[head % 2][...], values[head % 4][...])
        scaled = mixed * jnp.concatenate(inverse[head], axis=0)
        out_ref[:, head * VALUE_DIM : (head + 1) * VALUE_DIM] = scaled.astype(jnp.bfloat16)

    turns = TOKENS // SOFT
    cuts = POOL // CUT
    for stage in range(HEADS + 3):
        if 0 <= stage - 3 < HEADS:
            mix(stage - 3)
        for turn in range(turns):
            for cut in range(turn * cuts // turns, (turn + 1) * cuts // turns):
                if 0 <= stage - 1 < HEADS:
                    score(stage - 1, cut * CUT)
                if stage < HEADS:
                    make(stage, cut * CUT)
            if 0 <= stage - 2 < HEADS:
                soften(stage - 2, turn * SOFT)


def prefill(own, other, ready):
    return pl.pallas_call(
        prefill_kernel,
        out_shape=jax.ShapeDtypeStruct((TOKENS, HEADS * VALUE_DIM), jnp.bfloat16),
        in_specs=[vmem] * 3,
        out_specs=vmem,
        scratch_shapes=[
            pltpu.VMEM((POOL, LATENT), jnp.bfloat16),
            pltpu.VMEM((TOKENS, POOL), jnp.float32),
            *[pltpu.VMEM((POOL, DIRECT), jnp.bfloat16)] * 2,
            *[pltpu.VMEM((POOL, VALUE_DIM), jnp.bfloat16)] * 4,
            *[pltpu.VMEM((TOKENS, POOL), jnp.float32)] * 2,
            *[pltpu.VMEM((TOKENS, POOL), jnp.bfloat16)] * 2,
        ],
        compiler_params=params(PREFILL_MIB),
        cost_estimate=pl.CostEstimate(
            flops=2 * 2048 * 2048 * 1024, bytes_accessed=10_000_000, transcendentals=2048 * 2048
        ),
        name="prefill",
    )(own, other, ready)


def early_kernel(own, ready_hbm, weight_hbm, scores, ready, weight, keys, sems):
    loads = [
        pltpu.make_async_copy(ready_hbm.at[:NEWEST, :], ready.at[:NEWEST, :], sems.at[0]),
        pltpu.make_async_copy(ready_hbm.at[NEWEST:, :], ready.at[NEWEST:, :], sems.at[1]),
        pltpu.make_async_copy(weight_hbm.at[:EARLY, :], weight, sems.at[2]),
    ]
    for load in loads:
        load.start()
    unpack(own, keys, [keys], 0)
    loads[0].wait()
    rows = 2 * QUERIES
    for item in range(HEADS // 2):
        for at in range(0, HALF, DECODE_CUT):
            queries = ready[item * rows : (item + 1) * rows, :]
            scores[item, :, at : at + DECODE_CUT] = dot_t(queries, keys[at : at + DECODE_CUT, :])
    loads[1].wait()
    loads[2].wait()


def early(own, ready, out_weight):
    return pl.pallas_call(
        early_kernel,
        out_shape=(
            pltpu.VMEM((HEADS // 2, 2 * QUERIES, HALF), jnp.float32),
            pltpu.VMEM(ready.shape, ready.dtype),
            pltpu.VMEM((EARLY, MODEL), jnp.bfloat16),
        ),
        in_specs=[vmem, hbm, hbm],
        out_specs=(vmem,) * 3,
        scratch_shapes=[
            pltpu.VMEM((HALF, WIDTH), jnp.bfloat16),
            pltpu.SemaphoreType.DMA((3,)),
        ],
        compiler_params=params(EARLY_MIB),
        cost_estimate=pl.CostEstimate(
            flops=2 * 1024 * 1024 * 640, bytes_accessed=12_000_000, transcendentals=0
        ),
        name="early",
    )(own, ready, out_weight)


def decode_kernel(
    own, other, early, ready, first_weight, value_ref, weight_hbm,
    send_ref, heads_out, weight, sems, partial, keys, bias, s0, s1, w0, w1,
):
    core = own_core()
    loads = [
        pltpu.make_async_copy(
            weight_hbm.at[at : at + size, :], weight.at[at - EARLY : at - EARLY + size, :], sem
        )
        for at, size, sem in ((EARLY, 256, sems.at[0]), (EARLY + 256, 512, sems.at[1]))
    ]
    for load in loads:
        load.start()
    unpack(own, keys, [], 0)
    unpack(other, keys, [keys], HALF)
    keys[POOL:, :] = ready[NEWEST:BIAS, :]
    for at in range(0, KEYS, WIDTH):
        row = BIAS + at // WIDTH * QUERIES
        size = min(WIDTH, KEYS - at)
        bias[:, at : at + size] = ready[row : row + QUERIES, :size].astype(jnp.float32)
    scores, weights = (s0, s1), (w0, w1)
    inverse = {}
    items = HEADS // 2
    rows = 2 * QUERIES

    def score(item, at, size):
        queries = ready[item * rows : (item + 1) * rows, :]
        scores[item % 2][:, at - HALF : at - HALF + size] = dot_t(queries, keys[at : at + size, :])

    def soften(item, start):
        part = softmax_rows(
            [early.at[item], scores[item % 2]], bias, weights[item % 2], start, SOFT
        )
        inverse.setdefault(item, []).append(part)

    def mix(item):
        scale = jnp.concatenate(inverse[item], axis=0)
        mixed = [
            (dot(weights[item % 2][...], keys[:, at : at + 256]) * scale).astype(jnp.bfloat16)
            for at in range(0, LATENT, 256)
        ]
        mixed = jnp.concatenate(mixed, axis=1)
        for part in range(2):
            head = item * 2 + part
            columns = slice(head * VALUE_DIM, (head + 1) * VALUE_DIM)
            heads_out[:, columns] = dot(
                mixed[part * QUERIES : (part + 1) * QUERIES], value_ref[:, columns]
            ).astype(jnp.bfloat16)

    turns = rows // SOFT
    parts = [(at, min(DECODE_CUT, KEYS - at)) for at in range(HALF, KEYS, DECODE_CUT)]
    for stage in range(items + 2):
        if 0 <= stage - 2 < items:
            mix(stage - 2)
        if stage == items:
            loads[0].wait()
            for place in range(8):
                columns = columns_for(place, 1 - core)
                partial[place] = dot(heads_out[:, :EARLY], first_weight[:, columns]) + dot(
                    heads_out[:, EARLY : EARLY + 256], weight[:256, columns]
                )
        for turn in range(turns):
            if stage < items:
                for at, size in parts[turn * len(parts) // turns : (turn + 1) * len(parts) // turns]:
                    score(stage, at, size)
            if 0 <= stage - 1 < items:
                soften(stage - 1, turn * SOFT)
    loads[1].wait()
    for place in range(8):
        rest = dot(heads_out[:, EARLY + 256 :], weight[256:, columns_for(place, 1 - core)])
        send_ref[place] = turned(partial[place] + rest, 1 - core)


def columns_for(place, core):
    start = place * 2 * SHARE + core * (SHARE - 64)
    return pl.ds(pl.multiple_of(start, 128), SHARE + 64)


def turned(product, core):
    columns = product.T
    return jnp.where(core == 0, columns[:SHARE], columns[64:]).astype(jnp.bfloat16)


def keep_kernel(heads_out, first_weight, weight, keep_ref):
    core = own_core()
    for place in range(8):
        columns = columns_for(place, core)
        product = dot(heads_out[:, :EARLY], first_weight[:, columns])
        product = product + dot(heads_out[:, EARLY:], weight[:, columns])
        keep_ref[place] = turned(product, core)


def own_share(heads_out, first_weight, weight):
    return pl.pallas_call(
        keep_kernel,
        out_shape=jax.ShapeDtypeStruct((8, SHARE, QUERIES), jnp.bfloat16),
        in_specs=[vmem] * 3,
        out_specs=vmem,
        compiler_params=params(KEEP_MIB),
        cost_estimate=pl.CostEstimate(
            flops=2 * 128 * 1024 * 4096, bytes_accessed=8_000_000, transcendentals=0
        ),
        name="own_share",
    )(heads_out, first_weight, weight)


def decode(own, other, scores, ready, first_weight, absorb_values, out_weight):
    width = HEADS * VALUE_DIM
    return pl.pallas_call(
        decode_kernel,
        out_shape=(
            jax.ShapeDtypeStruct((8, SHARE, QUERIES), jnp.bfloat16),
            pltpu.VMEM((QUERIES, width), jnp.bfloat16),
            pltpu.VMEM((width - EARLY, MODEL), jnp.bfloat16),
        ),
        in_specs=[vmem] * 6 + [hbm],
        out_specs=(vmem,) * 3,
        scratch_shapes=[
            pltpu.SemaphoreType.DMA((2,)),
            pltpu.VMEM((8, QUERIES, SHARE + 64), jnp.float32),
            pltpu.VMEM((KEYS, WIDTH), jnp.bfloat16),
            pltpu.VMEM((QUERIES, KEYS), jnp.float32),
            pltpu.VMEM((2 * QUERIES, KEYS - HALF), jnp.float32),
            pltpu.VMEM((2 * QUERIES, KEYS - HALF), jnp.float32),
            pltpu.VMEM((2 * QUERIES, KEYS), jnp.bfloat16),
            pltpu.VMEM((2 * QUERIES, KEYS), jnp.bfloat16),
        ],
        compiler_params=params(DECODE_MIB),
        cost_estimate=pl.CostEstimate(
            flops=2 * 1024 * 2176 * 1280 + 2 * 128 * 1024 * 7168,
            bytes_accessed=22_000_000,
            transcendentals=1024 * 2176,
        ),
        name="decode",
    )(own, other, scores, ready, first_weight, absorb_values, out_weight)


def gather_sum_kernel(parts, out_ref):
    total = parts[0].astype(jnp.float32)
    for place in range(1, parts.shape[0]):
        total = total + parts[place].astype(jnp.float32)
    out_ref[...] = total.T.astype(jnp.bfloat16)


def gather_sum(parts):
    return pl.pallas_call(
        gather_sum_kernel,
        out_shape=jax.ShapeDtypeStruct((QUERIES, SHARE), jnp.bfloat16),
        in_specs=[vmem],
        out_specs=vmem,
        compiler_params=params(16),
        name="gather_sum",
    )(parts)


def on_device(
    pre_queries,
    pre_latent,
    absorb_keys,
    absorb_values,
    step_queries,
    step_latent,
    context_lengths,
    page_table,
    out_weight,
):
    pieces = pack(pre_latent).reshape(64, PIECE, 128)
    own = lax.all_to_all(pieces, BOTH, 0, 0, axis_index_groups=same_core_groups())
    own = own.reshape(32, 2 * PIECE, 128)
    ready, pre_ready = absorb(
        step_queries.reshape(QUERIES, HEADS * HEAD),
        absorb_keys,
        step_latent.reshape(QUERIES, LATENT + ROPE),
        context_lengths.reshape(ROWS, 1),
        page_table,
        pre_queries,
        absorb_values,
    )
    own, ready, pre_ready = lax.optimization_barrier((own, ready, pre_ready))
    other = lax.ppermute(own, BOTH, other_core())
    scores, ready, first_weight = early(own, ready, out_weight)
    send, heads_out, weight = decode(
        own, other, scores, ready, first_weight, absorb_values, out_weight
    )
    arrived = lax.ppermute(send, BOTH, other_core())
    keep = own_share(heads_out, first_weight, weight)
    chip = (keep.astype(jnp.float32) + arrived.astype(jnp.float32)).astype(jnp.bfloat16)
    chip, own, other = lax.optimization_barrier((chip, own, other))
    parts = lax.all_to_all(chip, BOTH, 0, 0, axis_index_groups=chip_groups())
    prefill_heads = prefill(own, other, pre_ready)
    decode_out = gather_sum(parts).reshape(STEPS, ROWS, SHARE)
    return (prefill_heads, decode_out)


def solution(mesh):
    return jax.shard_map(
        on_device,
        mesh=mesh,
        in_specs=(
            P("ctx", "tp"),
            P(("ctx", "tp"), None),
            P(None, "tp"),
            P(None, "tp"),
            P(None, "ctx", "tp"),
            P(None, "ctx", None),
            P("ctx"),
            P("ctx", None),
            P("tp", None),
        ),
        out_specs=(P("ctx", "tp"), P(None, "ctx", "tp")),
        check_vma=False,
    )
```

```python
import functools
import itertools
import math

import jax
import jax.numpy as jnp
from jax import lax
from jax.experimental import pallas as pl
from jax.experimental.pallas import tpu as pltpu
from jax.sharding import PartitionSpec as P

LATENT = 512
ROPE = 64
NOPE = 128
VALUE_DIM = 128
PAGE = 64
STEPS = 4
WIDTH = LATENT + 2 * ROPE
DIRECT = NOPE + 2 * ROPE
PIECE = 72
HALF = 1024
HEAD = NOPE + ROPE
HEADS = 8
TOKENS = 256
ROWS = 32
QUERIES = STEPS * ROWS
POOL = 2048
KEYS = POOL + QUERIES
MODEL = 7168
SHARE = 448
BOTH = ("ctx", "tp")
NEWEST = HEADS * QUERIES
BIAS = NEWEST + QUERIES

hidden = -1e30
CUT = 1024
SOFT = 16
DECODE_CUT = 256
PREFILL_MIB = 48
DECODE_MIB = 24
KEEP_MIB = 24
EARLY_MIB = 43
EARLY = 256
to_exp2 = math.log2(math.e) / math.sqrt(HEAD)
vmem = pl.BlockSpec(memory_space=pltpu.VMEM)
hbm = pl.BlockSpec(memory_space=pltpu.HBM)


def params(mib):
    return pltpu.CompilerParams(vmem_limit_bytes=mib * 1024 * 1024)


def flat(x, y, z, core):
    return (x * 2 + y // 2) * 16 + z * 4 + (y % 2) * 2 + core


def chips():
    return itertools.product(range(4), range(4), range(4), range(2))


def chip_groups():
    return [
        [flat(x, yh * 2 + yl, z, core) for z, yl in itertools.product(range(4), range(2))]
        for x, yh, core in itertools.product(range(4), range(2), range(2))
    ]


def other_core():
    return [(flat(x, y, z, c), flat(x, y, z, 1 - c)) for x, y, z, c in chips()]


def same_core_groups():
    return [
        [
            flat(x, yh * 2 + yl, z, core)
            for x, yh, z, yl in itertools.product(range(4), range(2), range(4), range(2))
        ]
        for core in range(2)
    ]


def own_core():
    return lax.axis_index("tp") % 2


def dot(a, b):
    return jnp.dot(a, b, preferred_element_type=jnp.float32)


def dot_t(a, b):
    return lax.dot_general(a, b, (((1,), (1,)), ((), ())), preferred_element_type=jnp.float32)


def pack_kernel(latent_ref, out_ref):
    late = (lax.axis_index("tp") // 2) % 2
    latent = latent_ref[...].astype(jnp.float32)
    rope = latent[:, LATENT:]
    parts = [latent[:, at : at + 128] for at in range(0, LATENT, 128)]
    rope = jnp.concatenate([rope[:8], rope[8:]], axis=1)
    piece = jnp.where(
        late == 0, jnp.concatenate([*parts, rope], axis=0), jnp.concatenate([rope, *parts], axis=0)
    )
    two = jnp.concatenate([piece, piece], axis=0).astype(jnp.bfloat16)
    for place in range(32):
        out_ref[place] = two


def pack(latent):
    return pl.pallas_call(
        pack_kernel,
        out_shape=jax.ShapeDtypeStruct((32, 2 * PIECE, 128), jnp.bfloat16),
        in_specs=[vmem],
        out_specs=vmem,
        compiler_params=params(16),
        name="pack",
    )(latent)


def unpack(source, latent, ropes, at):
    for pair in range(0, 32, 4):
        rows = slice(at + pair * 32, at + pair * 32 + 128)
        pairs = slice(pair, pair + 4)
        for tile in range(4):
            first = source[pairs, tile * 16 : (tile + 1) * 16, :]
            second = source[pairs, 80 + tile * 16 : 96 + tile * 16, :]
            latent[rows, tile * 128 : (tile + 1) * 128] = jnp.stack([first, second], axis=1).reshape(
                128, 128
            )
        rope = source[pairs, 64:80, :].astype(jnp.float32).reshape(8, 8, 128)
        left = lax.broadcasted_iota(jnp.int32, rope.shape, 2) < ROPE
        both = jnp.concatenate([jnp.where(left, rope, 0.0), jnp.where(left, 0.0, rope)], axis=1)
        both = both.reshape(128, 128).astype(jnp.bfloat16)
        for ref in ropes:
            ref[rows, ref.shape[1] - 2 * ROPE :] = both


def token_of_key(shape, dim, core):
    key = lax.broadcasted_iota(jnp.int32, shape, dim)
    row = key % HALF
    owner = jnp.where(key < HALF, core, 1 - core)
    return (row // 16) * 32 + owner * 16 + row % 16


def place_of_head(head):
    row = 2 * LATENT + head // 4 * TOKENS
    return slice(row, row + TOKENS), slice(head % 4 * DIRECT, (head % 4 + 1) * DIRECT)


def absorb_kernel(
    query_ref, key_ref, latent_ref, length_ref, table_ref, pre_ref, value_ref, out, pre_out
):
    core = own_core()
    pre_out[:LATENT, :] = key_ref[...]
    pre_out[LATENT : 2 * LATENT, :] = value_ref[...]
    for head in range(HEADS):
        query = pre_ref[:, head // 2 * 2 * HEAD : (head // 2 + 1) * 2 * HEAD]
        query = query[:, head % 2 * HEAD : (head % 2 + 1) * HEAD]
        rope = query[:, NOPE:]
        rows, columns = place_of_head(head)
        pre_out[rows, columns] = jnp.concatenate([query[:, :NOPE], rope, rope], axis=1)
    for pair in range(HEADS // 2):
        both = query_ref[:, pair * 2 * HEAD : (pair + 1) * 2 * HEAD]
        for part in range(2):
            head = pair * 2 + part
            query = both[:, part * HEAD : (part + 1) * HEAD]
            key_map = key_ref[:, head * NOPE : (head + 1) * NOPE]
            rows = slice(head * QUERIES, (head + 1) * QUERIES)
            out[rows, :LATENT] = dot_t(query[:, :NOPE], key_map).astype(jnp.bfloat16)
            rope = query[:, NOPE:]
            out[rows, LATENT:] = jnp.concatenate([rope, rope], axis=1)
    rows = slice(NEWEST, NEWEST + QUERIES)
    out[rows, : LATENT + ROPE] = latent_ref[...]
    out[rows, LATENT + ROPE :] = jnp.zeros((QUERIES, ROPE), jnp.bfloat16)
    table = table_ref[...]
    pages = table.shape[1]
    page = lax.broadcasted_iota(jnp.int32, table.shape, 1)
    slot = jnp.zeros(table.shape, jnp.int32)
    for place in range(pages):
        slot = slot + jnp.where(table[:, place : place + 1] == page, place, 0)
    limit = jnp.clip(length_ref[...] - slot * PAGE, 0, PAGE).astype(jnp.float32)
    shape = (pages, POOL)
    key = lax.broadcasted_iota(jnp.int32, shape, 1)
    of = (key % HALF) // (PAGE // 2)
    owner = (lax.broadcasted_iota(jnp.int32, shape, 0) == of).astype(jnp.bfloat16)
    spread = dot(limit.astype(jnp.bfloat16), owner)
    token = (token_of_key((ROWS, POOL), 1, core) % PAGE).astype(jnp.float32)
    pool = jnp.where(token < spread, 0.0, hidden)
    mine = lax.broadcasted_iota(jnp.int32, (QUERIES, QUERIES), 0)
    theirs = lax.broadcasted_iota(jnp.int32, (QUERIES, QUERIES), 1)
    seen = (mine % ROWS == theirs % ROWS) & (theirs // ROWS <= mine // ROWS)
    bias = jnp.concatenate([pool] * STEPS, axis=0)
    bias = jnp.concatenate([bias, jnp.where(seen, 0.0, hidden)], axis=1).astype(jnp.bfloat16)
    for at in range(0, KEYS, WIDTH):
        part = bias[:, at : at + WIDTH]
        row = BIAS + at // WIDTH * QUERIES
        out[row : row + QUERIES, : part.shape[1]] = part


def absorb(queries, absorb_keys, step_latent, lengths, table, pre_queries, absorb_values):
    return pl.pallas_call(
        absorb_kernel,
        out_shape=(
            jax.ShapeDtypeStruct((BIAS + 4 * QUERIES, WIDTH), jnp.bfloat16),
            jax.ShapeDtypeStruct((2 * LATENT + 2 * TOKENS, HEADS * NOPE), jnp.bfloat16),
        ),
        in_specs=[vmem] * 7,
        out_specs=(vmem, vmem),
        compiler_params=params(56),
        cost_estimate=pl.CostEstimate(
            flops=2 * 1024 * 128 * 512, bytes_accessed=5_000_000, transcendentals=0
        ),
        name="absorb",
    )(queries, absorb_keys, step_latent, lengths, table, pre_queries, absorb_values)


def softmax_rows(scores, bias, weights, start, count):
    bias_start = start % bias.shape[0]
    shifted = []
    at = 0
    for part in scores:
        size = part.shape[1]
        mask = bias[bias_start : bias_start + count, at : at + size]
        shifted.append(part[start : start + count, :] + mask)
        at += size
    largest = functools.reduce(
        jnp.maximum, [jnp.max(part, axis=1, keepdims=True) for part in shifted]
    )
    total = 0.0
    at = 0
    for part in shifted:
        expo = jnp.exp2(part * to_exp2 - largest * to_exp2)
        weights[start : start + count, at : at + part.shape[1]] = expo.astype(jnp.bfloat16)
        total = total + jnp.sum(expo, axis=1, keepdims=True)
        at += part.shape[1]
    return 1.0 / total


def prefill_kernel(own, other, ready, out_ref, latent, bias, *held):
    ctx, core = lax.axis_index("ctx"), own_core()
    keys, values, scores, weights = held[:2], held[2:6], held[6:8], held[8:]
    unpack(own, latent, keys, 0)
    unpack(other, latent, keys, HALF)
    token = token_of_key((TOKENS, POOL), 1, core)
    query = ctx * TOKENS + lax.broadcasted_iota(jnp.int32, (TOKENS, POOL), 0)
    bias[...] = jnp.where(token <= query, 0.0, hidden)
    inverse = {}

    def make(head, at):
        columns = slice(head * NOPE, (head + 1) * NOPE)
        maps = [ready[:LATENT, columns], ready[LATENT : 2 * LATENT, columns]]
        maps = jnp.concatenate(maps, axis=1)
        made = dot(latent[at : at + CUT, :], maps).astype(jnp.bfloat16)
        keys[head % 2][at : at + CUT, :NOPE] = made[:, :NOPE]
        values[head % 4][at : at + CUT, :] = made[:, NOPE:]

    def score(head, at):
        query = ready[place_of_head(head)]
        scores[head % 2][:, at : at + CUT] = dot_t(query, keys[head % 2][at : at + CUT, :])

    def soften(head, start):
        part = softmax_rows([scores[head % 2]], bias, weights[head % 2], start, SOFT)
        inverse.setdefault(head, []).append(part)

    def mix(head):
        mixed = dot(weights[head % 2][...], values[head % 4][...])
        scaled = mixed * jnp.concatenate(inverse[head], axis=0)
        out_ref[:, head * VALUE_DIM : (head + 1) * VALUE_DIM] = scaled.astype(jnp.bfloat16)

    turns = TOKENS // SOFT
    cuts = POOL // CUT
    for stage in range(HEADS + 3):
        if 0 <= stage - 3 < HEADS:
            mix(stage - 3)
        for turn in range(turns):
            for cut in range(turn * cuts // turns, (turn + 1) * cuts // turns):
                if 0 <= stage - 1 < HEADS:
                    score(stage - 1, cut * CUT)
                if stage < HEADS:
                    make(stage, cut * CUT)
            if 0 <= stage - 2 < HEADS:
                soften(stage - 2, turn * SOFT)


def prefill(own, other, ready):
    return pl.pallas_call(
        prefill_kernel,
        out_shape=jax.ShapeDtypeStruct((TOKENS, HEADS * VALUE_DIM), jnp.bfloat16),
        in_specs=[vmem] * 3,
        out_specs=vmem,
        scratch_shapes=[
            pltpu.VMEM((POOL, LATENT), jnp.bfloat16),
            pltpu.VMEM((TOKENS, POOL), jnp.float32),
            *[pltpu.VMEM((POOL, DIRECT), jnp.bfloat16)] * 2,
            *[pltpu.VMEM((POOL, VALUE_DIM), jnp.bfloat16)] * 4,
            *[pltpu.VMEM((TOKENS, POOL), jnp.float32)] * 2,
            *[pltpu.VMEM((TOKENS, POOL), jnp.bfloat16)] * 2,
        ],
        compiler_params=params(PREFILL_MIB),
        cost_estimate=pl.CostEstimate(
            flops=2 * 2048 * 2048 * 1024, bytes_accessed=10_000_000, transcendentals=2048 * 2048
        ),
        name="prefill",
    )(own, other, ready)


def early_kernel(own, ready_hbm, weight_hbm, scores, ready, weight, keys, sems):
    loads = [
        pltpu.make_async_copy(ready_hbm.at[:NEWEST, :], ready.at[:NEWEST, :], sems.at[0]),
        pltpu.make_async_copy(ready_hbm.at[NEWEST:, :], ready.at[NEWEST:, :], sems.at[1]),
        pltpu.make_async_copy(weight_hbm.at[:EARLY, :], weight, sems.at[2]),
    ]
    for load in loads:
        load.start()
    unpack(own, keys, [keys], 0)
    loads[0].wait()
    rows = 2 * QUERIES
    for item in range(HEADS // 2):
        for at in range(0, HALF, DECODE_CUT):
            queries = ready[item * rows : (item + 1) * rows, :]
            scores[item, :, at : at + DECODE_CUT] = dot_t(queries, keys[at : at + DECODE_CUT, :])
    loads[1].wait()
    loads[2].wait()


def early(own, ready, out_weight):
    return pl.pallas_call(
        early_kernel,
        out_shape=(
            pltpu.VMEM((HEADS // 2, 2 * QUERIES, HALF), jnp.float32),
            pltpu.VMEM(ready.shape, ready.dtype),
            pltpu.VMEM((EARLY, MODEL), jnp.bfloat16),
        ),
        in_specs=[vmem, hbm, hbm],
        out_specs=(vmem,) * 3,
        scratch_shapes=[
            pltpu.VMEM((HALF, WIDTH), jnp.bfloat16),
            pltpu.SemaphoreType.DMA((3,)),
        ],
        compiler_params=params(EARLY_MIB),
        cost_estimate=pl.CostEstimate(
            flops=2 * 1024 * 1024 * 640, bytes_accessed=12_000_000, transcendentals=0
        ),
        name="early",
    )(own, ready, out_weight)


def decode_kernel(
    own, other, early, ready, first_weight, value_ref, weight_hbm,
    send_ref, heads_out, weight, sems, partial, keys, bias, s0, s1, w0, w1,
):
    core = own_core()
    loads = [
        pltpu.make_async_copy(
            weight_hbm.at[at : at + size, :], weight.at[at - EARLY : at - EARLY + size, :], sem
        )
        for at, size, sem in ((EARLY, 256, sems.at[0]), (EARLY + 256, 512, sems.at[1]))
    ]
    for load in loads:
        load.start()
    unpack(own, keys, [], 0)
    unpack(other, keys, [keys], HALF)
    keys[POOL:, :] = ready[NEWEST:BIAS, :]
    for at in range(0, KEYS, WIDTH):
        row = BIAS + at // WIDTH * QUERIES
        size = min(WIDTH, KEYS - at)
        bias[:, at : at + size] = ready[row : row + QUERIES, :size].astype(jnp.float32)
    scores, weights = (s0, s1), (w0, w1)
    inverse = {}
    items = HEADS // 2
    rows = 2 * QUERIES

    def score(item, at, size):
        queries = ready[item * rows : (item + 1) * rows, :]
        scores[item % 2][:, at - HALF : at - HALF + size] = dot_t(queries, keys[at : at + size, :])

    def soften(item, start):
        part = softmax_rows(
            [early.at[item], scores[item % 2]], bias, weights[item % 2], start, SOFT
        )
        inverse.setdefault(item, []).append(part)

    def mix(item):
        scale = jnp.concatenate(inverse[item], axis=0)
        mixed = [
            (dot(weights[item % 2][...], keys[:, at : at + 256]) * scale).astype(jnp.bfloat16)
            for at in range(0, LATENT, 256)
        ]
        mixed = jnp.concatenate(mixed, axis=1)
        for part in range(2):
            head = item * 2 + part
            columns = slice(head * VALUE_DIM, (head + 1) * VALUE_DIM)
            heads_out[:, columns] = dot(
                mixed[part * QUERIES : (part + 1) * QUERIES], value_ref[:, columns]
            ).astype(jnp.bfloat16)

    turns = rows // SOFT
    parts = [(at, min(DECODE_CUT, KEYS - at)) for at in range(HALF, KEYS, DECODE_CUT)]
    for stage in range(items + 2):
        if 0 <= stage - 2 < items:
            mix(stage - 2)
        if stage == items:
            loads[0].wait()
            for place in range(8):
                columns = columns_for(place, 1 - core)
                partial[place] = dot(heads_out[:, :EARLY], first_weight[:, columns]) + dot(
                    heads_out[:, EARLY : EARLY + 256], weight[:256, columns]
                )
        for turn in range(turns):
            if stage < items:
                for at, size in parts[turn * len(parts) // turns : (turn + 1) * len(parts) // turns]:
                    score(stage, at, size)
            if 0 <= stage - 1 < items:
                soften(stage - 1, turn * SOFT)
    loads[1].wait()
    for place in range(8):
        rest = dot(heads_out[:, EARLY + 256 :], weight[256:, columns_for(place, 1 - core)])
        send_ref[place] = turned(partial[place] + rest, 1 - core)


def columns_for(place, core):
    start = place * 2 * SHARE + core * (SHARE - 64)
    return pl.ds(pl.multiple_of(start, 128), SHARE + 64)


def turned(product, core):
    columns = product.T
    return jnp.where(core == 0, columns[:SHARE], columns[64:]).astype(jnp.bfloat16)


def keep_kernel(heads_out, first_weight, weight, keep_ref):
    core = own_core()
    for place in range(8):
        columns = columns_for(place, core)
        product = dot(heads_out[:, :EARLY], first_weight[:, columns])
        product = product + dot(heads_out[:, EARLY:], weight[:, columns])
        keep_ref[place] = turned(product, core)


def own_share(heads_out, first_weight, weight):
    return pl.pallas_call(
        keep_kernel,
        out_shape=jax.ShapeDtypeStruct((8, SHARE, QUERIES), jnp.bfloat16),
        in_specs=[vmem] * 3,
        out_specs=vmem,
        compiler_params=params(KEEP_MIB),
        cost_estimate=pl.CostEstimate(
            flops=2 * 128 * 1024 * 4096, bytes_accessed=8_000_000, transcendentals=0
        ),
        name="own_share",
    )(heads_out, first_weight, weight)


def decode(own, other, scores, ready, first_weight, absorb_values, out_weight):
    width = HEADS * VALUE_DIM
    return pl.pallas_call(
        decode_kernel,
        out_shape=(
            jax.ShapeDtypeStruct((8, SHARE, QUERIES), jnp.bfloat16),
            pltpu.VMEM((QUERIES, width), jnp.bfloat16),
            pltpu.VMEM((width - EARLY, MODEL), jnp.bfloat16),
        ),
        in_specs=[vmem] * 6 + [hbm],
        out_specs=(vmem,) * 3,
        scratch_shapes=[
            pltpu.SemaphoreType.DMA((2,)),
            pltpu.VMEM((8, QUERIES, SHARE + 64), jnp.float32),
            pltpu.VMEM((KEYS, WIDTH), jnp.bfloat16),
            pltpu.VMEM((QUERIES, KEYS), jnp.float32),
            pltpu.VMEM((2 * QUERIES, KEYS - HALF), jnp.float32),
            pltpu.VMEM((2 * QUERIES, KEYS - HALF), jnp.float32),
            pltpu.VMEM((2 * QUERIES, KEYS), jnp.bfloat16),
            pltpu.VMEM((2 * QUERIES, KEYS), jnp.bfloat16),
        ],
        compiler_params=params(DECODE_MIB),
        cost_estimate=pl.CostEstimate(
            flops=2 * 1024 * 2176 * 1280 + 2 * 128 * 1024 * 7168,
            bytes_accessed=22_000_000,
            transcendentals=1024 * 2176,
        ),
        name="decode",
    )(own, other, scores, ready, first_weight, absorb_values, out_weight)


def add_kernel(a_ref, b_ref, out_ref):
    for place in range(8):
        both = a_ref[place].astype(jnp.float32) + b_ref[place].astype(jnp.float32)
        out_ref[place] = both.astype(jnp.bfloat16)


def add_shares(a, b):
    return pl.pallas_call(
        add_kernel,
        out_shape=jax.ShapeDtypeStruct(a.shape, a.dtype),
        in_specs=[vmem] * 2,
        out_specs=vmem,
        compiler_params=params(16),
        name="add_shares",
    )(a, b)


def gather_sum_kernel(parts, out_ref):
    total = parts[0].astype(jnp.float32)
    for place in range(1, parts.shape[0]):
        total = total + parts[place].astype(jnp.float32)
    out_ref[...] = total.T.astype(jnp.bfloat16)


def gather_sum(parts):
    return pl.pallas_call(
        gather_sum_kernel,
        out_shape=jax.ShapeDtypeStruct((QUERIES, SHARE), jnp.bfloat16),
        in_specs=[vmem],
        out_specs=vmem,
        compiler_params=params(16),
        name="gather_sum",
    )(parts)


def on_device(
    pre_queries,
    pre_latent,
    absorb_keys,
    absorb_values,
    step_queries,
    step_latent,
    context_lengths,
    page_table,
    out_weight,
):
    pieces = pack(pre_latent).reshape(64, PIECE, 128)
    own = lax.all_to_all(pieces, BOTH, 0, 0, axis_index_groups=same_core_groups())
    own = own.reshape(32, 2 * PIECE, 128)
    ready, pre_ready = absorb(
        step_queries.reshape(QUERIES, HEADS * HEAD),
        absorb_keys,
        step_latent.reshape(QUERIES, LATENT + ROPE),
        context_lengths.reshape(ROWS, 1),
        page_table,
        pre_queries,
        absorb_values,
    )
    own, ready, pre_ready = lax.optimization_barrier((own, ready, pre_ready))
    other = lax.ppermute(own, BOTH, other_core())
    scores, ready, first_weight = early(own, ready, out_weight)
    send, heads_out, weight = decode(
        own, other, scores, ready, first_weight, absorb_values, out_weight
    )
    arrived = lax.ppermute(send, BOTH, other_core())
    keep = own_share(heads_out, first_weight, weight)
    chip = add_shares(keep, arrived)
    chip, own, other = lax.optimization_barrier((chip, own, other))
    parts = lax.all_to_all(chip, BOTH, 0, 0, axis_index_groups=chip_groups())
    prefill_heads = prefill(own, other, pre_ready)
    decode_out = gather_sum(parts).reshape(STEPS, ROWS, SHARE)
    return (prefill_heads, decode_out)


def solution(mesh):
    return jax.shard_map(
        on_device,
        mesh=mesh,
        in_specs=(
            P("ctx", "tp"),
            P(("ctx", "tp"), None),
            P(None, "tp"),
            P(None, "tp"),
            P(None, "ctx", "tp"),
            P(None, "ctx", None),
            P("ctx"),
            P("ctx", None),
            P("tp", None),
        ),
        out_specs=(P("ctx", "tp"), P(None, "ctx", "tp")),
        check_vma=False,
    )
```
